128 devices in a mesh: dp: 16 (over z, y_lo, core), mp: 8 (over x, y_hi).
Axes of the slice: x: 4, y: 4 (y_hi: 2, y_lo: 2; y = y_hi * 2 + y_lo), z: 4, core: 2. Of those that a mesh axis runs over, the one named last changes fastest.
Arguments:
- tokens: float32 [20480, 1152], P(('dp', 'mp')), may hold values from -6 to 6
- cotangent: float32 [20480, 1152], P(('dp', 'mp')), may hold values from -6 to 6
- time_embed: float32 [32, 1152], replicated, may hold values from -6 to 6
- attend_weight: bfloat16 [1, 3, 1152, 1152], P(None, None, 'dp', 'mp'), may hold values from -0.1875 to 0.1875
- time_weight: bfloat16 [1, 2, 1152, 1152], P(None, None, 'dp', 'mp'), may hold values from -0.1875 to 0.1875
- out_weight: bfloat16 [1, 1152, 1152], P(None, 'mp', 'dp'), may hold values from -0.75 to 0.75
- expand_weight: bfloat16 [1, 4608, 1152], P(None, 'mp', 'dp'), may hold values from -0.1875 to 0.1875
- reduce_weight: bfloat16 [1, 4608, 1152], P(None, 'mp', 'dp'), may hold values from -0.09375 to 0.09375
- row_params: bfloat16 [1, 6, 1152], P(None, None, 'dp')
- expand_bias: float32 [1, 4608], P(None, 'mp'), may hold values from -3 to 3
- bias_table: float32 [1, 16, 1521], P(None, 'mp'), may hold values from -4 to 4
- grid_height: int32 [64], P('dp'), may hold values from 12 to 20, as said below
- grid_width: int32 [64], P('dp'), may hold values from 12 to 20
- group_count: int32 [16], P('dp'), may hold values from 1 to 4, as said below
- group_bucket: int32 [16], P('dp'), may hold values from 0 to 31
- shares: int32 [16], replicated, may hold values from 1 to 8
Outputs:
- output: float32 [20480, 1152], P(('dp', 'mp'))
- grad_tokens: float32 [20480, 1152], P(('dp', 'mp'))
- grad_attend: float32 [1, 3, 1152, 1152], P(None, None, 'dp', 'mp')
- grad_time: float32 [1, 2, 1152, 1152], P(None, None, 'dp', 'mp')
- grad_out: float32 [1, 1152, 1152], P(None, 'mp', 'dp')
- grad_expand: float32 [1, 4608, 1152], P(None, 'mp', 'dp')
- grad_reduce: float32 [1, 4608, 1152], P(None, 'mp', 'dp')
- grad_rows: float32 [1, 6, 1152], P(None, None, 'dp')
- grad_expand_bias: float32 [1, 4608], P(None, 'mp')
- grad_table: float32 [1, 16, 1521], P(None, 'mp')
The draws below stay inside these ranges and needn't reach their ends.
Inputs may be any that keep to these rules, and one draw needn't show every extreme that they name: Each image's grid_height * grid_width lies between 192 and 320; some image has height 12 and some height 20. `group_count`: some group is full.
All inputs are finite; a program needn't handle non-finite values.
Results may differ from the reference program's by a relative error of at most 0.025.
Values may be sent and summed in bfloat16 or wider, within the bound.
A program may use at most 448 MiB of HBM per device.

```python
import jax
import jax.numpy as jnp
from jax import lax

D = 1152
HEADS = 16
HEAD_DIM = 72
FF = 4608
LAYERS = 1
SLOTS = 4
PAD = 320
GRID_MIN = 12
GRID_MAX = 20
LEN_MIN = 192
BUCKETS = 32
GROUPS = 16
IMAGES = 64
TOKENS = 20480
REL = 1521


def grid_pair(key):
    heights = jax.random.randint(jax.random.fold_in(key, 11), (IMAGES,), GRID_MIN, GRID_MAX + 1)
    lower_width = jnp.maximum(GRID_MIN, (LEN_MIN + heights - 1) // heights)
    upper_width = jnp.minimum(GRID_MAX, PAD // heights)
    widths = jax.random.randint(jax.random.fold_in(key, 12), (IMAGES,), lower_width, upper_width + 1)
    chosen = jax.random.randint(jax.random.fold_in(key, 13), (), 0, IMAGES - 1)
    heights = heights.at[chosen].set(GRID_MIN).at[chosen + 1].set(GRID_MAX)
    widths = widths.at[chosen].set(min(GRID_MAX, PAD // GRID_MIN)).at[chosen + 1].set(PAD // GRID_MAX)
    return (heights.astype(jnp.int32), widths.astype(jnp.int32))


def draw_grid_height(key, part):
    heights, widths = grid_pair(key)
    return heights


def draw_grid_width(key, part):
    heights, widths = grid_pair(key)
    return widths


def draw_group_count(key, part):
    key = jax.random.fold_in(key, 3)
    counts = jax.random.randint(key, (GROUPS,), 1, SLOTS + 1)
    filled = jax.random.randint(jax.random.fold_in(key, 5), (), 0, GROUPS)
    return counts.at[filled].set(SLOTS).astype(jnp.int32)


def draw_row_params(key, part):
    key = jax.random.fold_in(key, 4)
    gains = 1.0 + 0.5 * jax.random.uniform(jax.random.fold_in(key, 6), (LAYERS, 6, D), jnp.float32, -1.0, 1.0)
    offsets = 0.5 * jax.random.normal(jax.random.fold_in(key, 7), (LAYERS, 6, D), jnp.float32)
    kinds = jnp.arange(6)
    is_gain = (kinds == 0) | (kinds == 3)
    values = jnp.where(is_gain[None, :, None], gains, offsets)
    return values.astype(jnp.bfloat16)


def plant(values, own_key, least, high):
    extent = values.shape
    index_at = [jax.random.randint(jax.random.fold_in(own_key, axis), (), 0, extent[axis]) for axis in range(len(extent))]
    values = values.at[tuple(index_at)].set(least)
    longest = extent.index(max(extent))
    index_at[longest] = (index_at[longest] + 1) % extent[longest]
    return values.at[tuple(index_at)].set(high)


def steps_of(rng, shape, pieces, smallest, high):
    loudness, own = 1.0, jax.random.fold_in(rng, 6)
    for axis_at, parts in pieces:
        steps = jnp.exp(jax.random.uniform(jax.random.fold_in(own, axis_at), (parts,), jnp.float32, smallest / len(pieces), high / len(pieces)))
        loudness = loudness * jnp.repeat(steps, shape[axis_at] // parts).reshape([-1 if axis == axis_at else 1 for axis in range(len(shape))])
    return loudness


def normal_values(rng, extent, deviation, limit, split=(), kind=jnp.bfloat16):
    values = deviation * jax.random.normal(rng, extent, jnp.float32)
    if split:
        values = values * steps_of(rng, extent, split, -0.22, 0.18)
    return jnp.clip(values, -limit, limit).astype(kind)


def setup_inputs(seed: int = 0) -> dict:
    key_list = jax.random.split(jax.random.key(seed), 17)
    return {
        "tokens": normal_values(key_list[0], (TOKENS, D), 1.0, 6.0, ((0, 128),), jnp.float32),
        "cotangent": normal_values(key_list[1], (TOKENS, D), 1.0, 6.0, ((0, 128),), jnp.float32),
        "time_embed": normal_values(key_list[2], (BUCKETS, D), 1.0, 6.0, (), jnp.float32),
        "attend_weight": normal_values(key_list[3], (LAYERS, 3, D, D), D ** -0.5, 0.1875, ((2, 16), (3, 8))),
        "time_weight": normal_values(key_list[4], (LAYERS, 2, D, D), D ** -0.5, 0.1875, ((2, 16), (3, 8))),
        "out_weight": normal_values(key_list[5], (LAYERS, D, D), (D // 16) ** -0.5, 0.75, ((1, 8), (2, 16))),
        "expand_weight": normal_values(key_list[6], (LAYERS, FF, D), D ** -0.5, 0.1875, ((1, 8), (2, 16))),
        "reduce_weight": normal_values(key_list[7], (LAYERS, FF, D), FF ** -0.5, 0.09375, ((1, 8), (2, 16))),
        "row_params": draw_row_params(jax.random.fold_in(key_list[16], 71), 0),
        "expand_bias": normal_values(key_list[9], (LAYERS, FF), 0.5, 3.0, ((1, 8),), jnp.float32),
        "bias_table": normal_values(key_list[10], (LAYERS, HEADS, REL), 1.0, 4.0, ((1, 8),), jnp.float32),
        "grid_height": draw_grid_height(jax.random.fold_in(key_list[16], 71), 0),
        "grid_width": draw_grid_width(jax.random.fold_in(key_list[16], 71), 0),
        "group_count": draw_group_count(jax.random.fold_in(key_list[16], 71), 0),
        "group_bucket": plant(jax.random.randint(key_list[14], (GROUPS,), 0, BUCKETS), jax.random.fold_in(key_list[14], 1), 0, BUCKETS - 1).astype(jnp.int32),
        "shares": plant(jax.random.randint(key_list[15], (GROUPS,), 1, 9), jax.random.fold_in(key_list[15], 1), 1, 8).astype(jnp.int32),
    }


@jax.custom_vjp
def low(v):
    return lax.optimization_barrier(v.astype(jnp.bfloat16)).astype(jnp.float32)

@jax.custom_vjp
def low_back(v):
    return v

def low_keep(v):
    return (low(v), None)

def low_pass(kept, grad):
    return (grad,)

def back_keep(v):
    return (v, None)

def back_low(kept, grad):
    return (low(grad),)
low.defvjp(low_keep, low_pass)
low_back.defvjp(back_keep, back_low)
EPSILON = 1e-06
MASKED = -1e+30
HIGHEST = lax.Precision.HIGHEST

def matmul(left, right):
    return jnp.dot(left, right, precision=HIGHEST)

def layer_norm(values, norm_gain, offset):
    row_mean = lax.optimization_barrier(jnp.mean(values, axis=-1, keepdims=True))
    centred = values - row_mean
    spread = lax.optimization_barrier(jnp.mean(centred * centred, axis=-1, keepdims=True))
    return centred * lax.rsqrt(spread + EPSILON) * norm_gain + offset

def grid_index(height, grid_width):
    position = jnp.arange(PAD, dtype=jnp.int32)
    grid_row = position // grid_width
    grid_col = position % grid_width
    side = 2 * GRID_MAX - 1
    rel_index = (grid_row[:, None] - grid_row[None, :] + (GRID_MAX - 1)) * side + (grid_col[:, None] - grid_col[None, :] + (GRID_MAX - 1))
    return jnp.clip(rel_index, 0, side * side - 1).astype(jnp.int32)

def group_layers(residual, time_row, lengths, heights, widths, params):
    attend_all, time_all, out_all, expand_all, reduce_all, rows_all, expand_bias_all, table_all = params
    total_rows = SLOTS * PAD
    key_valid = jnp.arange(PAD, dtype=jnp.int32)[None, :] < lengths[:, None]
    rel_index = jax.vmap(grid_index)(heights, widths)
    time_low = low(time_row)
    scale = HEAD_DIM ** (-0.5)
    shape4 = (SLOTS, PAD, HEADS, HEAD_DIM)
    for layer_pos in range(LAYERS):
        rows_now = rows_all[layer_pos]
        normed = low(layer_norm(residual, rows_now[0], rows_now[1]))
        query_bias = matmul(time_low[None, :], time_all[layer_pos, 0])
        value_bias = matmul(time_low[None, :], time_all[layer_pos, 1])
        queries = low(low_back(matmul(normed, attend_all[layer_pos, 0]) + query_bias))
        key_rows = low(low_back(matmul(normed, attend_all[layer_pos, 1])))
        values = low(low_back(matmul(normed, attend_all[layer_pos, 2])))
        scores = jnp.einsum('sqhe,skhe->shqk', queries.reshape(shape4), key_rows.reshape(shape4), precision=HIGHEST) * scale
        table_bias = jnp.take(table_all[layer_pos], rel_index, axis=1)
        scores = low_back(scores + jnp.transpose(table_bias, (1, 0, 2, 3)))
        scores = jnp.where(key_valid[:, None, None, :], scores, MASKED)
        weights_low = low(jax.nn.softmax(scores, axis=-1))
        mixed = jnp.einsum('shqk,skhe->sqhe', weights_low, values.reshape(shape4), precision=HIGHEST).reshape(total_rows, D)
        mixed = low(low_back(mixed + value_bias))
        branch = low_back(matmul(mixed, out_all[layer_pos]) + rows_now[2])
        residual = residual + branch
        normed = low(layer_norm(residual, rows_now[3], rows_now[4]))
        hidden = low_back(matmul(normed, expand_all[layer_pos].T) + expand_bias_all[layer_pos])
        activated = low(jax.nn.gelu(hidden, approximate=True))
        branch = low_back(matmul(activated, reduce_all[layer_pos]) + rows_now[5])
        residual = residual + branch
    valid_rows = key_valid.reshape(total_rows).astype(jnp.float32)
    return residual * valid_rows[:, None]

def reference(tokens, cotangent, time_embed, attend_weight, time_weight, out_weight, expand_weight, reduce_weight, row_params, expand_bias, bias_table, grid_height, grid_width, group_count, group_bucket, shares):
    params = (attend_weight.astype(jnp.float32), time_weight.astype(jnp.float32), out_weight.astype(jnp.float32), expand_weight.astype(jnp.float32), reduce_weight.astype(jnp.float32), row_params.astype(jnp.float32), expand_bias.astype(jnp.float32), bias_table.astype(jnp.float32))
    total_rows = SLOTS * PAD
    residual_groups = tokens.reshape(GROUPS, total_rows, D)
    slot_ids = jnp.arange(SLOTS, dtype=jnp.int32)
    heights = grid_height.reshape(GROUPS, SLOTS)
    widths = grid_width.reshape(GROUPS, SLOTS)
    lengths = heights * widths * (slot_ids[None, :] < group_count[:, None]).astype(jnp.int32)
    times = time_embed[group_bucket]
    share_f = shares.astype(jnp.float32)
    weight = share_f * GROUPS / jnp.sum(share_f)
    weighted = cotangent.reshape(GROUPS, total_rows, D) * weight[:, None, None]

    def forward(residual_all, weights_all):

        def one_group(item):
            residual, time_row, length_row, height_row, width_row = item
            return group_layers(residual, time_row, length_row, height_row, width_row, weights_all)
        return lax.map(jax.checkpoint(one_group), (residual_all, times, lengths, heights, widths))
    result, pull = jax.vjp(forward, residual_groups, params)
    grad_input, grad_params = pull(weighted)
    return (result.reshape(TOKENS, D), grad_input.reshape(TOKENS, D), grad_params[0], grad_params[1], grad_params[2], grad_params[3], grad_params[4], grad_params[5], grad_params[6], grad_params[7])
```

```python
import functools
from functools import partial

import jax
import jax.numpy as jnp
from jax import lax
from jax.experimental import pallas as pl
from jax.experimental.pallas import tpu as pltpu
from jax.sharding import Mesh
from jax.sharding import PartitionSpec as P

HEAD_DIM = 72
LAYERS = 1
SLOTS = 4
PAD = 320
GRID_MAX = 20
MP = ("mp_0", "mp_1")
DP_MP = ("dp", "mp_0", "mp_1")


EPSILON = 1e-06
MASKED = -1e30


def gathered_by_axis(x, axes, dim):
    if not axes:
        return x
    nearer = lax.all_gather(x, axes[-1], axis=dim, tiled=True)
    return gathered_by_axis(nearer, axes[:-1], dim)


def summed_rows(terms, axes):
    subtotal = terms.astype(jnp.bfloat16)
    for axis in axes:
        subtotal = lax.psum_scatter(subtotal, axis, scatter_dimension=0, tiled=True)
    return subtotal.astype(jnp.float32)


def gather_turned(arrays, axis, dims):
    turned = [jnp.moveaxis(a, dim, 0) for a, dim in zip(arrays, dims)]
    widths = [t[0].size for t in turned]
    both = jnp.concatenate([t.reshape(-1, w) for t, w in zip(turned, widths)], axis=1)
    filled = lax.all_gather(both, axis, axis=0, tiled=True)
    pieces = jnp.split(filled, [sum(widths[:k]) for k in range(1, len(widths))], axis=1)
    return tuple(
        (
            jnp.moveaxis(b.reshape(-1, *t.shape[1:]), 0, dim)
            for b, t, dim in zip(pieces, turned, dims)
        )
    )


def in_one_piece(arrays, axis, dim, along):
    both = jnp.concatenate(arrays, axis=along)
    filled, at, finished = (lax.psum_scatter(both, axis, scatter_dimension=dim, tiled=True), 0, [])
    for a in arrays:
        finished.append(lax.slice_in_dim(filled, at, at + a.shape[along], axis=along))
        at += a.shape[along]
    return tuple(finished)


def sent_to_all(x, axis):
    count = lax.axis_size(axis)
    return lax.all_to_all(jnp.broadcast_to(x[None], (count, *x.shape)), axis, 0, 0, tiled=True)


def taken_together(x, axis):
    return sent_to_all(x, axis).sum(axis=0)


def together(arrays, axis):
    ends = [0]
    for a in arrays:
        ends.append(ends[-1] + a.size)
    subtotal = taken_together(jnp.concatenate([a.ravel() for a in arrays]), axis)
    return tuple((subtotal[b:e].reshape(a.shape) for a, b, e in zip(arrays, ends, ends[1:])))


CELLS=400; SIDE=20; HD=72; SCALE=72**-0.5
bf=jnp.bfloat16; f32=jnp.float32

def cell_maps(h, w, live):
    a=lax.broadcasted_iota(jnp.int32,(CELLS,PAD),0)
    r=(a*3277)>>16
    c=a-r*SIDE
    ok=(r<h)&(c<w)&live
    p=lax.broadcasted_iota(jnp.int32,(CELLS,PAD),1)
    to_cells=jnp.where(ok&(r*w+c==p),1.0,0.0).astype(bf)
    a=lax.broadcasted_iota(jnp.int32,(PAD,CELLS),1)
    r=(a*3277)>>16
    c=a-r*SIDE
    ok=(r<h)&(c<w)&live
    p=lax.broadcasted_iota(jnp.int32,(PAD,CELLS),0)
    to_rows=jnp.where(ok&(r*w+c==p),1.0,0.0).astype(bf)
    return to_cells,to_rows

def key_mask(h,w,live):
    a=lax.broadcasted_iota(jnp.int32,(1,CELLS),1)
    r=(a*3277)>>16
    c=a-r*SIDE
    return jnp.where((r<h)&(c<w)&live,0.0,-1e30)

def dotnt(a,b): return lax.dot_general(a,b,(((1,),(1,)),((),())),preferred_element_type=f32)
def dottn(a,b): return lax.dot_general(a,b,(((0,),(0,)),((),())),preferred_element_type=f32)
def dot(a,b): return jnp.dot(a,b,preferred_element_type=f32)

def fwd_kernel(H, hw_ref, strip_ref, q_ref, k_ref, v_ref, o_ref, p_ref, b_ref):
    s=pl.program_id(0)
    @pl.when(s==0)
    def _():
        for hd in range(H):
            for i in range(SIDE):
                off=SIDE*(SIDE-1-i)
                b_ref[hd,SIDE*i:SIDE*i+SIDE,:]=strip_ref[hd,:,off:off+CELLS]
    h=hw_ref[0,s]; w=hw_ref[1,s]; live=hw_ref[2,s]>0
    to_cells,to_rows=cell_maps(h,w,live)
    mask=key_mask(h,w,live)
    qg=dot(to_cells,q_ref[...]).astype(bf)
    kg=dot(to_cells,k_ref[...]).astype(bf)
    vg=dot(to_cells,v_ref[...]).astype(bf)
    outs=[]
    for hd in range(H):
        sl=slice(hd*HD,hd*HD+HD)
        sc=dotnt(qg[:,sl],kg[:,sl])*SCALE+b_ref[hd]+mask
        m=jnp.max(sc,axis=-1,keepdims=True)
        e=jnp.exp(sc-m)
        p=(e*(1.0/jnp.sum(e,axis=-1,keepdims=True))).astype(bf)
        p_ref[0,hd]=p
        outs.append(dot(p,vg[:,sl]).astype(bf))
    o_ref[...]=dot(to_rows,jnp.concatenate([o.astype(f32) for o in outs],axis=1).astype(bf))

def attn_fwd(q,k,v,strip,hw):
    S=hw.shape[1]; H=q.shape[1]//HD
    spec=pl.BlockSpec((PAD,H*HD),lambda s:(s,0))
    return pl.pallas_call(functools.partial(fwd_kernel,H),grid=(S,),
        out_shape=(jax.ShapeDtypeStruct(q.shape,f32),jax.ShapeDtypeStruct((S,H,CELLS,CELLS),bf)),
        in_specs=[pl.BlockSpec(memory_space=pltpu.SMEM),pl.BlockSpec(strip.shape,lambda s:(0,0,0)),spec,spec,spec],
        out_specs=(spec,pl.BlockSpec((1,H,CELLS,CELLS),lambda s:(s,0,0,0))),
        scratch_shapes=[pltpu.VMEM((H,CELLS,CELLS),f32)],
        compiler_params=pltpu.CompilerParams(vmem_limit_bytes=48*2**20))(hw,strip,q,k,v)

def bwd_kernel(H, hw_ref, p_ref, do_ref, q_ref, k_ref, v_ref, dq_ref, dk_ref, dv_ref, gs_ref, g_ref):
    s=pl.program_id(0)
    @pl.when(s==0)
    def _():
        g_ref[...]=jnp.zeros_like(g_ref)
    h=hw_ref[0,s]; w=hw_ref[1,s]; live=hw_ref[2,s]>0
    to_cells,to_rows=cell_maps(h,w,live)
    qg=dot(to_cells,q_ref[...]).astype(bf)
    kg=dot(to_cells,k_ref[...]).astype(bf)
    vg=dot(to_cells,v_ref[...]).astype(bf)
    dg=dot(to_cells,do_ref[...]).astype(bf)
    dqs,dks,dvs=[],[],[]
    for hd in range(H):
        sl=slice(hd*HD,hd*HD+HD)
        p=p_ref[0,hd]
        pf=p.astype(f32)
        dp=dotnt(dg[:,sl],vg[:,sl])
        ds=(pf*(dp-jnp.sum(dp*pf,axis=-1,keepdims=True))).astype(bf)
        g_ref[hd]+=ds.astype(f32)
        dqs.append(dot(ds,kg[:,sl])*SCALE)
        dks.append(dottn(ds,qg[:,sl])*SCALE)
        dvs.append(dottn(p,dg[:,sl]))
    for ref,parts in ((dq_ref,dqs),(dk_ref,dks),(dv_ref,dvs)):
        ref[...]=dot(to_rows,jnp.concatenate(parts,axis=1).astype(bf)).astype(bf)
    @pl.when(s==pl.num_programs(0)-1)
    def _():
        gs_ref[...]=jnp.zeros_like(gs_ref)
        for hd in range(H):
            for i in range(SIDE):
                off=SIDE*(SIDE-1-i)
                gs_ref[hd,:,off:off+CELLS]+=g_ref[hd,SIDE*i:SIDE*i+SIDE,:]

def attn_bwd(p,do,q,k,v,hw):
    S=hw.shape[1]; H=q.shape[1]//HD
    spec=pl.BlockSpec((PAD,H*HD),lambda s:(s,0))
    o=jax.ShapeDtypeStruct(q.shape,bf)
    return pl.pallas_call(functools.partial(bwd_kernel,H),grid=(S,),
        out_shape=(o,o,o,jax.ShapeDtypeStruct((H,SIDE,780),f32)),
        in_specs=[pl.BlockSpec(memory_space=pltpu.SMEM),pl.BlockSpec((1,H,CELLS,CELLS),lambda s:(s,0,0,0)),spec,spec,spec,spec],
        out_specs=(spec,spec,spec,pl.BlockSpec((H,SIDE,780),lambda s:(0,0,0))),
        scratch_shapes=[pltpu.VMEM((H,CELLS,CELLS),f32)],
        compiler_params=pltpu.CompilerParams(vmem_limit_bytes=48*2**20))(hw,p,do,q,k,v)

def strip_of(table):
    t=table.reshape(-1,39,39)[:,::-1,::-1]
    return jnp.stack([t[:,:,19-j:39-j] for j in range(SIDE)],axis=1).reshape(-1,SIDE,780)

def table_of(strip):
    s=strip.reshape(-1,SIDE,39,SIDE)
    t=sum(jnp.pad(s[:,j],((0,0),(0,0),(19-j,j))) for j in range(SIDE))
    return t[:,::-1,::-1].reshape(-1,1521)


def layer_norm(values, norm_gain, offset):
    row_mean = jnp.mean(values, axis=-1, keepdims=True)
    centred = values - row_mean
    spread = jnp.mean(centred * centred, axis=-1, keepdims=True)
    return centred * lax.rsqrt(spread + EPSILON) * norm_gain + offset


def gelu_tanh(values):
    return jax.nn.gelu(values, approximate=True)


def grid_index(height, grid_width):
    position = jnp.arange(PAD, dtype=jnp.int32)
    grid_row = position // grid_width
    grid_col = position % grid_width
    side = 2 * GRID_MAX - 1
    rel_index = (grid_row[:, None] - grid_row[None, :] + (GRID_MAX - 1)) * side + (
        grid_col[:, None] - grid_col[None, :] + (GRID_MAX - 1)
    )
    return jnp.clip(rel_index, 0, side * side - 1)


def gather_rows(block):
    return gathered_by_axis(block, MP, 0)


def spread_sum(term_fn, own_rows):
    return summed_rows(term_fn(jnp.int32(0), own_rows * lax.axis_size(MP)), MP)


def layer_weights(
    attend_weight, time_weight, out_weight, expand_weight, reduce_weight, row_params, layer_pos
):
    return gather_turned(
        (
            attend_weight[layer_pos],
            time_weight[layer_pos],
            out_weight[layer_pos],
            expand_weight[layer_pos],
            reduce_weight[layer_pos],
            row_params[layer_pos],
        ),
        "dp",
        (1, 1, 1, 1, 1, 1),
    )


def rows_product(left, right, first_row, row_count):
    return jnp.dot(left, right, preferred_element_type=jnp.float32)


def triple_product(triple, weights, first_row, row_count):
    return jnp.einsum("cre,cde->rd", triple, weights, preferred_element_type=jnp.float32)


def project(full_rows, attend_mat, time_mat, time_low):
    projected = jnp.einsum("rd,cde->cre", full_rows, attend_mat, preferred_element_type=jnp.float32)
    query_bias = jnp.dot(time_low[None, :], time_mat[0], preferred_element_type=jnp.float32)
    value_bias = jnp.dot(time_low[None, :], time_mat[1], preferred_element_type=jnp.float32)
    queries = (projected[0] + query_bias).astype(jnp.bfloat16)
    return (
        queries,
        projected[1].astype(jnp.bfloat16),
        projected[2].astype(jnp.bfloat16),
        value_bias,
    )


def position_bias(table, rel_index):
    return jnp.transpose(jnp.take(table, rel_index, axis=1), (1, 0, 2, 3))


def score_block(queries, key_rows, bias4, key_valid):
    shape4 = (SLOTS, PAD, bias4.shape[1], HEAD_DIM)
    scores = jnp.einsum(
        "sqhe,skhe->shqk",
        queries.reshape(shape4),
        key_rows.reshape(shape4),
        preferred_element_type=jnp.float32,
    ) * HEAD_DIM ** (-0.5)
    scores = scores + bias4
    return jnp.where(key_valid[:, None, None, :], scores, MASKED)


def mix_values(weights_low, values, value_bias):
    shape4 = (SLOTS, PAD, values.shape[1] // HEAD_DIM, HEAD_DIM)
    mixed = jnp.einsum(
        "shqk,skhe->sqhe", weights_low, values.reshape(shape4), preferred_element_type=jnp.float32
    )
    return (mixed.reshape(values.shape) + value_bias).astype(jnp.bfloat16)


def body(
    tokens,
    cotangent,
    time_embed,
    attend_weight,
    time_weight,
    out_weight,
    expand_weight,
    reduce_weight,
    row_params,
    expand_bias,
    bias_table,
    grid_height,
    grid_width,
    group_count,
    group_bucket,
    shares,
):
    own_rows = tokens.shape[0]
    total_rows = SLOTS * PAD
    first_own = lax.axis_index(MP) * own_rows
    slot_ids = jnp.arange(SLOTS, dtype=jnp.int32)
    lengths = grid_height * grid_width * (slot_ids < group_count[0]).astype(jnp.int32)
    key_valid = jnp.arange(PAD, dtype=jnp.int32)[None, :] < lengths[:, None]
    valid_own = lax.dynamic_slice_in_dim(
        key_valid.reshape(total_rows).astype(jnp.float32), first_own, own_rows, 0
    )
    time_low = lax.dynamic_index_in_dim(time_embed, group_bucket[0], 0, keepdims=False).astype(
        jnp.bfloat16
    )
    time_f = time_low.astype(jnp.float32)
    share_f = shares.astype(jnp.float32)
    weight = share_f[lax.axis_index("dp")] * share_f.shape[0] / jnp.sum(share_f)
    hw = jnp.stack([grid_height, grid_width, (slot_ids < group_count[0]).astype(jnp.int32)])
    residual = tokens
    gathered = layer_weights(
        attend_weight, time_weight, out_weight, expand_weight, reduce_weight, row_params, 0
    )
    attend_mat, time_mat, out_mat, expand_mat, reduce_mat, rows_mat = gathered
    rows_f = rows_mat.astype(jnp.float32)
    normed_f, norm_back_one = jax.vjp(layer_norm, residual, rows_f[0], rows_f[1])
    full_rows_one = gather_rows(normed_f.astype(jnp.bfloat16))
    queries, key_rows, values, value_bias = project(full_rows_one, attend_mat, time_mat, time_low)
    mixed, probs = attn_fwd(queries, key_rows, values, strip_of(bias_table[0]), hw)
    mixed = (mixed + value_bias).astype(jnp.bfloat16)
    residual = residual + spread_sum(partial(rows_product, mixed, out_mat), own_rows) + rows_f[2]
    normed_f, norm_back_two = jax.vjp(layer_norm, residual, rows_f[3], rows_f[4])
    full_rows = gather_rows(normed_f.astype(jnp.bfloat16))
    hidden = (
        jnp.einsum("rd,fd->rf", full_rows, expand_mat, preferred_element_type=jnp.float32)
        + expand_bias[0]
    )
    activated_f, gelu_back = jax.vjp(gelu_tanh, hidden)
    activated = activated_f.astype(jnp.bfloat16)
    residual = (
        residual + spread_sum(partial(rows_product, activated, reduce_mat), own_rows) + rows_f[5]
    )
    output = residual * valid_own[:, None]
    grad_residual = cotangent * weight * valid_own[:, None]
    results = []
    for layer_pos in reversed(range(LAYERS)):
        grad_full = gather_rows(grad_residual.astype(jnp.bfloat16))
        bias_two = jnp.sum(grad_full.astype(jnp.float32), axis=0)
        grad_reduce = jnp.einsum(
            "rf,rd->fd", activated, grad_full, preferred_element_type=jnp.float32
        )
        grad_active = jnp.einsum(
            "rd,fd->rf", grad_full, reduce_mat, preferred_element_type=jnp.float32
        )
        grad_hidden = gelu_back(grad_active)[0].astype(jnp.bfloat16)
        grad_expand_bias = jnp.sum(grad_hidden.astype(jnp.float32), axis=0)
        grad_expand = jnp.einsum(
            "rf,rd->fd", grad_hidden, full_rows, preferred_element_type=jnp.float32
        )
        grad_normed = spread_sum(partial(rows_product, grad_hidden, expand_mat), own_rows)
        grad_middle, gain_two, offset_two = norm_back_two(grad_normed)
        grad_middle = grad_middle + grad_residual
        full_rows = full_rows_one
        norm_back = norm_back_one
        grad_full = gather_rows(grad_middle.astype(jnp.bfloat16))
        bias_out = jnp.sum(grad_full.astype(jnp.float32), axis=0)
        grad_out = jnp.einsum("re,rd->ed", mixed, grad_full, preferred_element_type=jnp.float32)
        grad_mixed = jnp.einsum(
            "rd,ed->re", grad_full, out_mat, preferred_element_type=jnp.float32
        ).astype(jnp.bfloat16)
        grad_queries, grad_keys, grad_values, grad_strip = attn_bwd(
            probs, grad_mixed, queries, key_rows, values, hw
        )
        grad_table = table_of(grad_strip)
        grad_triple = jnp.stack([grad_queries, grad_keys, grad_values])
        grad_attend = jnp.einsum(
            "rd,cre->cde", full_rows, grad_triple, preferred_element_type=jnp.float32
        )
        grad_time = jnp.stack(
            [
                time_f[:, None] * jnp.sum(grad_queries.astype(jnp.float32), axis=0)[None, :],
                time_f[:, None] * jnp.sum(grad_mixed.astype(jnp.float32), axis=0)[None, :],
            ]
        )
        grad_normed = spread_sum(partial(triple_product, grad_triple, attend_mat), own_rows)
        grad_input, gain_one, offset_one = norm_back(grad_normed)
        grad_residual = grad_input + grad_middle
        norm_sums = lax.psum(jnp.stack([gain_one, offset_one, gain_two, offset_two]), MP)
        rows_grad = jnp.stack(
            [norm_sums[0], norm_sums[1], bias_out, norm_sums[2], norm_sums[3], bias_two]
        )
        shards = (
            *tuple(
                (
                    part.astype(jnp.float32)
                    for part in in_one_piece(
                        (grad_attend.astype(jnp.bfloat16), grad_time.astype(jnp.bfloat16)),
                        "dp",
                        1,
                        0,
                    )
                )
            ),
            *tuple(
                (
                    part.astype(jnp.float32)
                    for part in in_one_piece(
                        (
                            grad_out.astype(jnp.bfloat16),
                            grad_expand.astype(jnp.bfloat16),
                            grad_reduce.astype(jnp.bfloat16),
                            rows_grad.astype(jnp.bfloat16),
                        ),
                        "dp",
                        1,
                        0,
                    )
                )
            ),
        )
        bias_sums = together((grad_expand_bias, grad_table), "dp")
        results.append(tuple(shards) + tuple(bias_sums))
    ordered = results[::-1]
    stacked = [jnp.stack([entry[member] for entry in ordered]) for member in range(8)]
    return (
        output,
        grad_residual,
        stacked[0],
        stacked[1],
        stacked[2],
        stacked[3],
        stacked[4],
        stacked[5],
        stacked[6],
        stacked[7],
    )


def solution(mesh):
    torus = Mesh(mesh.devices.reshape(mesh.shape["dp"], 4, 2), ("dp", "mp_0", "mp_1"))
    in_specs = (
        P(DP_MP, None),
        P(DP_MP, None),
        P(),
        P(None, None, "dp", MP),
        P(None, None, "dp", MP),
        P(None, MP, "dp"),
        P(None, MP, "dp"),
        P(None, MP, "dp"),
        P(None, None, "dp"),
        P(None, MP),
        P(None, MP, None),
        P("dp"),
        P("dp"),
        P("dp"),
        P("dp"),
        P(),
    )
    out_specs = (
        P(DP_MP, None),
        P(DP_MP, None),
        P(None, None, "dp", MP),
        P(None, None, "dp", MP),
        P(None, MP, "dp"),
        P(None, MP, "dp"),
        P(None, MP, "dp"),
        P(None, None, "dp"),
        P(None, MP),
        P(None, MP, None),
    )
    return jax.shard_map(body, mesh=torus, in_specs=in_specs, out_specs=out_specs, check_vma=False)
```

```python
import functools

import jax
import jax.numpy as jnp
from jax import lax
from jax.experimental import pallas as pl
from jax.experimental.pallas import tpu as pltpu
from jax.sharding import Mesh
from jax.sharding import PartitionSpec as P

AXES = ("z", "yl", "c", "x", "yh")
SIZES = {"z": 4, "yl": 2, "c": 2, "x": 4, "yh": 2}
DP = ("z", "yl", "c")
MP = ("x", "yh")

D = 1152
HD = 72
PAD = 320
OWN = 160
ROWS = 640
SIDE = 20
CELLS = 400
STRIP = 896
SCALE = 72**-0.5
EPSILON = 1e-06
MASKED = -1e30
UNIT = 144
HALF = 512
LANE_O = 216
LANE_T = 288
LANE_P = 432
LANE_E = 448

bf = jnp.bfloat16
f32 = jnp.float32


def dot(a, b):
    return jnp.dot(a, b, preferred_element_type=f32)


def dot_nt(a, b):
    return lax.dot_general(a, b, (((1,), (1,)), ((), ())), preferred_element_type=f32)


def dot_tn(a, b):
    return lax.dot_general(a, b, (((0,), (0,)), ((), ())), preferred_element_type=f32)


def normalised(values):
    centred = values - jnp.mean(values, axis=-1, keepdims=True)
    rstd = lax.rsqrt(jnp.mean(centred * centred, axis=-1, keepdims=True) + EPSILON)
    return centred * rstd, rstd


def norm_back(grad, gain, unit, rstd):
    scaled = grad * gain
    inner = jnp.mean(scaled, axis=-1, keepdims=True)
    along = jnp.mean(scaled * unit, axis=-1, keepdims=True)
    return rstd * (scaled - inner - unit * along)


def gelu_pair(h):
    k0 = 0.7978845608028654
    k1 = 0.044715
    sq = h * h
    t = jnp.tanh(k0 * h * (1.0 + k1 * sq))
    half = 0.5 * (1.0 + t)
    slope = half + 0.5 * h * (1.0 - t * t) * (k0 * (1.0 + 3.0 * k1 * sq))
    return h * half, slope


def cell_maps(height, width, live, to_cells, to_rows, mask):
    def cells(shape, dim):
        a = lax.broadcasted_iota(jnp.int32, shape, dim)
        r = (a * 3277) >> 16
        c = a - r * SIDE
        return r.astype(f32), c.astype(f32)

    def hot(shape, cell_dim):
        r, c = cells(shape, cell_dim)
        p = lax.broadcasted_iota(jnp.int32, shape, 1 - cell_dim).astype(f32)
        hit = (r < height) & (c < width) & (live > 0.5) & (r * width + c == p)
        return jnp.where(hit, 1.0, 0.0).astype(bf)

    r, c = cells((1, CELLS), 1)
    mask[...] = jnp.where((r < height) & (c < width) & (live > 0.5), 0.0, MASKED)
    to_cells[...] = hot((CELLS, PAD), 0)
    to_rows[...] = hot((PAD, CELLS), 1)


class Wire:
    def __init__(self, sends, recvs):
        self.sends, self.recvs, self.used = sends, recvs, 0

    def copy(self, src, dst, **steps):
        at = self.used
        self.used += 1
        return pltpu.make_async_remote_copy(
            src_ref=src,
            dst_ref=dst,
            send_sem=self.sends.at[at],
            recv_sem=self.recvs.at[at],
            device_id=away(**steps),
            device_id_type=pl.DeviceIdType.MESH,
        )


def away(**steps):
    return {a: lax.rem(lax.axis_index(a) + s, SIZES[a]) for a, s in steps.items()}


def signal(semaphore, steps):
    pl.semaphore_signal(
        semaphore, inc=1, device_id=away(**steps), device_id_type=pl.DeviceIdType.MESH
    )


def start(copies):
    for one in copies:
        one.start()


def recv(copies):
    for one in copies:
        one.wait_recv()


def drain(copies):
    for one in copies:
        one.wait_send()


N_SEMS = 104


def layer_kernel(
    pack_a,
    pack_m,
    tok_ref,
    cot_ref,
    info_in,
    scal_ref,
    strip_in,
    out_ref,
    gtok_ref,
    fin_a,
    fin_m,
    fin_small,
    fin_rows,
    wa,
    wm,
    in_pack_a,
    in_pack_m,
    info,
    strips,
    f_a,
    f_m,
    f_c,
    f_g,
    to_cells,
    to_rows,
    masks,
    cells,
    probs,
    bias,
    mixed,
    dqkv,
    tsum,
    we,
    wr,
    act,
    gh,
    totals,
    cut_sib,
    cut_yh,
    got_sib,
    got_yh,
    cut_sib2,
    cut_yh2,
    got_sib2,
    got_yh2,
    got_x4,
    got_z4,
    got_z1,
    got_x1,
    got_yl,
    small,
    got_small,
    rgrad,
    got_rg,
    got_rg7,
    sends,
    recvs,
    credit,
    local,
):
    z, yl, c, x, yh = (lax.axis_index(a) for a in AXES)
    wire = Wire(sends, recvs)
    own_at = pl.multiple_of((2 * c + yh) * OWN, OWN)
    yhp_at = pl.multiple_of((2 * c + 1 - yh) * OWN, OWN)
    own_rows = pl.ds(own_at, OWN)
    yhp_rows = pl.ds(yhp_at, OWN)
    other_group = pl.ds(pl.multiple_of((1 - c) * PAD, PAD), PAD)
    own_group = pl.ds(pl.multiple_of(c * PAD, PAD), PAD)
    near_half = pl.ds(pl.multiple_of(yh * OWN, OWN), OWN)
    far_half = pl.ds(pl.multiple_of((1 - yh) * OWN, OWN), OWN)

    part, part2 = totals.at[0], totals.at[1]
    x_steps = [dict(x=s) for s in (1, 2, 3)]
    z_steps = [dict(z=s) for s in (1, 2, 3)]
    y_steps = [dict(yl=a, c=b, yh=d) for a in (0, 1) for b in (0, 1) for d in (0, 1) if a + b + d]
    barrier = pltpu.get_barrier_semaphore()
    for steps in x_steps + z_steps + y_steps:
        signal(barrier, steps)
    pl.semaphore_wait(barrier, 13)

    class Gather:
        def __init__(self, pack, landing, weights):
            self.pack, self.landing, self.w = pack, landing, weights
            self.sib = wire.copy(pack.at[1 - c], landing, c=1)
            own = weights.at[x, z, yl]
            self.low = wire.copy(own, own, yl=1)
            a, b = weights.at[x, z, 0], weights.at[x, z, 1]
            self.one = (
                [wire.copy(a, a, **s) for s in z_steps],
                [wire.copy(b, b, **s) for s in x_steps],
            )
            a, b = weights.at[x, :, 0], weights.at[:, z, 1]
            self.two = (
                [wire.copy(a, a, **s) for s in x_steps],
                [wire.copy(b, b, **s) for s in z_steps],
            )

        def unit(self):
            self.sib.wait_recv()
            mine = self.pack[c].astype(f32)
            other = self.landing[...].astype(f32)
            first = jnp.where(c == 0, mine, other)[:HD]
            second = jnp.where(c == 0, other, mine)[:HD]
            self.w[x, z, yl] = jnp.concatenate([first, second], axis=0).astype(bf)
            self.low.start()

            @pl.when(yl == 0)
            def _():
                start(self.one[0])

            @pl.when(yl == 1)
            def _():
                start(self.one[1])

        def other_unit(self):
            self.low.wait_recv()

            @pl.when(yl == 0)
            def _():
                start(self.one[1])

            @pl.when(yl == 1)
            def _():
                start(self.one[0])

        def spread(self, kind):
            recv(self.one[kind])
            start(self.two[kind])

        def end(self):
            recv(self.two[0] + self.two[1])
            drain([self.sib, self.low, *self.one[0], *self.one[1], *self.two[0], *self.two[1]])

    class Rows:
        def __init__(self, full):
            own, far = full.at[own_rows], full.at[yhp_rows]
            self.yh = wire.copy(own, own, yh=1)
            self.sib = wire.copy(own, own, c=1)
            self.fwd = wire.copy(far, far, c=1)

        def start(self):
            start([self.yh, self.sib])

        def pass_on(self):
            self.yh.wait_recv()
            self.fwd.start()

        def end(self):
            recv([self.sib, self.fwd])
            drain([self.sib, self.fwd, self.yh])

    class Sums:
        def __init__(self, total, cut_s, cut_y, got_s, got_y):
            self.total, self.cut_s, self.cut_y = total, cut_s, cut_y
            self.got_s, self.got_y = got_s, got_y
            self.sib = wire.copy(cut_s, got_s, c=1)
            self.yh = wire.copy(cut_y, got_y, yh=1)

        def pass_on(self):
            self.sib.wait_recv()
            far = self.total[far_half] + self.got_s[far_half].astype(f32)
            self.cut_y[...] = far.astype(bf)
            self.yh.start()

        def end(self):
            self.yh.wait_recv()
            own = self.total[near_half] + self.got_s[near_half].astype(f32)
            drain([self.sib, self.yh])
            return own + self.got_y[...].astype(f32)

    class Scatter:
        def __init__(self, grads, final, got_low):
            self.g, self.final, self.got_low = grads, final, got_low
            self.one = (
                [wire.copy(grads.at[lax.rem(x + s, 4), :, 0], got_x4.at[s - 1], x=s) for s in (1, 2, 3)],
                [wire.copy(grads.at[:, lax.rem(z + s, 4), 1], got_z4.at[s - 1], z=s) for s in (1, 2, 3)],
            )
            self.two = (
                [wire.copy(grads.at[x, lax.rem(z + s, 4), 0], got_z1.at[s - 1], z=s) for s in (1, 2, 3)],
                [wire.copy(grads.at[lax.rem(x + s, 4), z, 1], got_x1.at[s - 1], x=s) for s in (1, 2, 3)],
            )
            self.low = wire.copy(grads.at[x, z, 1 - yl], got_low, yl=1)
            self.sib = wire.copy(final.at[c], final.at[c], c=1)

        def first(self):
            start(self.one[0] + self.one[1])

        def second(self):
            recv(self.one[0])

            def add0(k, carry):
                total = self.g[x, k, 0].astype(f32)
                for s in range(3):
                    total = total + got_x4[s, k].astype(f32)
                self.g[x, k, 0] = total.astype(bf)
                return carry

            lax.fori_loop(0, 4, add0, 0)
            start(self.two[0])
            recv(self.one[1])

            def add1(k, carry):
                total = self.g[k, z, 1].astype(f32)
                for s in range(3):
                    total = total + got_z4[s, k].astype(f32)
                self.g[k, z, 1] = total.astype(bf)
                return carry

            lax.fori_loop(0, 4, add1, 0)
            start(self.two[1])

        def third(self):
            recv(self.two[0] + self.two[1])
            for t, got in ((0, got_z1), (1, got_x1)):
                total = self.g[x, z, t].astype(f32)
                for s in range(3):
                    total = total + got[s].astype(f32)
                self.g[x, z, t] = total.astype(bf)
            self.low.start()

        def fourth(self):
            self.low.wait_recv()
            self.final[c] = self.g[x, z, yl].astype(f32) + self.got_low[...].astype(f32)
            self.sib.start()

        def end(self):
            self.sib.wait_recv()
            drain([*self.one[0], *self.one[1], *self.two[0], *self.two[1], self.low, self.sib])

    w_a = Gather(pack_a, in_pack_a, wa)
    w_m = Gather(pack_m, in_pack_m, wm)
    rows_a, rows_c, rows_m, rows_g = Rows(f_a), Rows(f_c), Rows(f_m), Rows(f_g)
    info_copy = wire.copy(info.at[c], info.at[c], c=1)
    strip_copies = [wire.copy(strips.at[x], strips.at[x], **s) for s in x_steps]

    start([w_a.sib, w_m.sib])
    cot_copy = pltpu.make_async_copy(cot_ref, gtok_ref, local)
    cot_copy.start()
    height, width, live = (scal_ref[0:1, k : k + 1] for k in (0, 1, 2))
    share = scal_ref[0:1, 3:4]
    info[c] = info_in[...]
    info_copy.start()
    strips[x] = strip_in[...]
    w_a.unit()
    unit_a, _ = normalised(tok_ref[...])
    f_a[own_rows] = unit_a.astype(bf)
    rows_a.start()
    start(strip_copies)
    w_a.other_unit()
    position = lax.broadcasted_iota(jnp.int32, (OWN, 1), 0).astype(f32)
    position = position + (yh * OWN).astype(f32)
    valid = jnp.where((position < height * width) & (live > 0.5), 1.0, 0.0)
    cot_copy.wait()
    gtok_ref[...] = gtok_ref[...] * share * valid
    f_c[own_rows] = gtok_ref[...].astype(bf)
    w_a.spread(0)
    w_a.spread(1)
    w_m.unit()
    rows_a.pass_on()
    rows_c.start()

    recv(strip_copies)
    drain(strip_copies)

    def build_bias(hd, carry):
        for i in range(SIDE):
            off = SIDE * (SIDE - 1 - i)
            bias[hd, SIDE * i : SIDE * i + SIDE, :] = strips[hd, 0:SIDE, off : off + CELLS]
        return carry

    lax.fori_loop(0, 4, build_bias, 0)
    info_copy.wait_recv()
    for g in (0, 1):
        cell_maps(
            *(info[g, 1:2, k : k + 1].astype(f32) for k in (0, 1, 2)),
            to_cells.at[g],
            to_rows.at[g],
            masks.at[g],
        )
    w_m.other_unit()
    rows_a.end()
    w_a.end()
    w_m.spread(0)
    w_m.spread(1)
    rows_c.pass_on()

    row_id = lax.broadcasted_iota(jnp.int32, (16, 128), 0)
    lane_id = lax.broadcasted_iota(jnp.int32, (16, 128), 1)
    pick = jnp.where(lane_id == row_id + (LANE_P - 384), 1.0, 0.0).astype(bf)
    params = dot_nt(pick, wa[0].reshape(D, HALF)[:, 384:512])
    par = [params[k : k + 1] for k in range(6)]

    def gain_rows(i, carry):
        at = pl.ds(pl.multiple_of(i * 64, 64), 64)
        f_a[at] = (f_a[at].astype(f32) * par[0] + par[1]).astype(bf)
        return carry

    lax.fori_loop(0, ROWS // 64, gain_rows, 0)

    lanes256 = lax.broadcasted_iota(jnp.int32, (1, 256), 1)
    time_rows = info[...].reshape(32, D)

    def head_forward(hd, carry):
        w_head = wa[hd].reshape(D, HALF)
        timed = pltpu.roll(dot(time_rows, w_head[:, 256:512]), 256 - 32, axis=1)
        qkv = dot(f_a[...], w_head[:, 0:256])
        for g in (0, 1):
            time_g = timed[16 * g : 16 * g + 1]
            low = (qkv[PAD * g : PAD * g + PAD] + jnp.where(lanes256 < HD, time_g, 0.0)).astype(bf)
            cell = dot(to_cells[g], low).astype(bf)
            cells[2 * hd + g] = cell
            score = dot_nt(cell[:, 0:HD], cell[:, HD : 2 * HD]) * SCALE + bias[hd] + masks[g]
            score = jnp.exp(score - jnp.max(score, axis=-1, keepdims=True))
            prob = (score * (1.0 / jnp.sum(score, axis=-1, keepdims=True))).astype(bf)
            probs[2 * hd + g] = prob
            o = dot(to_rows[g], dot(prob, cell[:, 2 * HD : 3 * HD]).astype(bf))
            mixed[hd, PAD * g : PAD * g + PAD, :] = (o + time_g[:, HD : 2 * HD]).astype(bf)
        return carry

    lax.fori_loop(0, 4, head_forward, 0)
    rows_c.end()

    def out_project(at):
        total = jnp.zeros((PAD, D), f32)
        for hd in range(4):
            w_out = wa[hd].reshape(D, HALF)[:, LANE_O:LANE_T]
            total = total + dot_nt(mixed[hd, at], w_out)
        return total

    attn_sum = Sums(part, cut_sib, cut_yh, got_sib, got_yh)
    cut_sib[...] = out_project(other_group).astype(bf)
    attn_sum.sib.start()
    part[...] = out_project(own_group)
    attn_sum.pass_on()
    w_m.end()

    for hd in range(4):
        p, at = hd // 2, 288 * (hd % 2)
        we[p, :, at : at + 64] = wa[hd].reshape(D, HALF)[:, LANE_E:HALF]
        we[p, :, at + 64 : at + 288] = wm[hd].reshape(D, HALF)[:, 0:224]
        wr[p, :, at : at + 288] = wm[hd].reshape(D, HALF)[:, 224:512]
    out_ref[...] = tok_ref[...] + par[2] + attn_sum.end()
    unit_m, _ = normalised(out_ref[...])
    f_m[own_rows] = (unit_m * par[3] + par[4]).astype(bf)
    rows_m.start()
    rows_m.pass_on()
    rows_m.end()

    def mlp(at):
        total = jnp.zeros((PAD, D), f32)
        for p in (0, 1):
            hidden_bias = jnp.concatenate([strips[2 * p + k, 24:25, 0:288] for k in (0, 1)], axis=1)
            value, slope = gelu_pair(dot(f_m[at], we[p]) + hidden_bias)
            act[p, at] = value.astype(bf)
            low = (dot(f_c[at], wr[p]) * slope).astype(bf)
            gh[p, at] = low
            total = total + dot_nt(low, we[p])
        return total

    mlp_grad = Sums(part, cut_sib, cut_yh, got_sib, got_yh)
    cut_sib[...] = mlp(other_group).astype(bf)
    mlp_grad.sib.start()
    part[...] = mlp(own_group)
    mlp_grad.pass_on()

    def mlp_out(at):
        return dot_nt(act[0, at], wr[0]) + dot_nt(act[1, at], wr[1])

    mlp_sum = Sums(part2, cut_sib2, cut_yh2, got_sib2, got_yh2)
    cut_sib2[...] = mlp_out(other_group).astype(bf)
    mlp_sum.sib.start()
    part2[...] = mlp_out(own_group)

    small[...] = jnp.zeros_like(small)
    ones = jnp.ones((16, ROWS), bf)
    for p in (0, 1):
        bias_sum = dot(ones, gh[p])
        grad_e = dot_tn(f_m[...], gh[p]).astype(bf).reshape(4, 2, UNIT, 576)
        for k in (0, 1):
            hd, at = 2 * p + k, 288 * k
            small[hd, 24:25, 0:288] = bias_sum[0:1, at : at + 288]
            wa[hd, :, :, :, LANE_E:HALF] = grad_e[:, :, :, at : at + 64]
            wm[hd, :, :, :, 0:224] = grad_e[:, :, :, at + 64 : at + 288]
        grad_r = dot_tn(f_c[...], act[p]).astype(bf).reshape(4, 2, UNIT, 576)
        for k in (0, 1):
            hd, at = 2 * p + k, 288 * k
            wm[hd, :, :, :, 224:512] = grad_r[:, :, :, at : at + 288]
    sc_m = Scatter(wm, fin_m, got_yl.at[0])
    sc_m.first()

    unit_m, rstd_m = normalised(out_ref[...])
    gy = mlp_grad.end()
    rgrad[...] = jnp.zeros_like(rgrad)
    rgrad[3:4] = jnp.sum(gy * unit_m, axis=0, keepdims=True)
    rgrad[4:5] = jnp.sum(gy, axis=0, keepdims=True)
    rgrad[5:6] = jnp.sum(f_c[own_rows].astype(f32), axis=0, keepdims=True)
    gtok_ref[...] = gtok_ref[...] + norm_back(gy, par[3], unit_m, rstd_m)
    low_mid = gtok_ref[...].astype(bf)
    rgrad[2:3] = jnp.sum(low_mid.astype(f32), axis=0, keepdims=True)
    f_g[own_rows] = low_mid
    rows_g.start()
    mlp_sum.pass_on()
    rows_g.pass_on()
    bias[...] = jnp.zeros_like(bias)
    rows_g.end()

    def head_backward(hd, carry):
        w_head = wa[hd].reshape(D, HALF)
        gmix = dot(f_g[...], w_head[:, 128:384])[:, LANE_O - 128 : LANE_T - 128].astype(bf)
        time_sums = []
        for g in (0, 1):
            mine = gmix[PAD * g : PAD * g + PAD]
            dcell = dot(to_cells[g], mine).astype(bf)
            cell = cells[2 * hd + g]
            prob = probs[2 * hd + g]
            wide = prob.astype(f32)
            dprob = dot_nt(dcell, cell[:, 2 * HD : 3 * HD])
            ds = (wide * (dprob - jnp.sum(dprob * wide, axis=-1, keepdims=True))).astype(bf)
            bias[hd] += ds.astype(f32)
            dq = dot(ds, cell[:, HD : 2 * HD]) * SCALE
            dk = dot_tn(ds, cell[:, 0:HD]) * SCALE
            dv = dot_tn(prob, dcell)
            packed = jnp.concatenate([dq, dk, dv, jnp.zeros((CELLS, 40), f32)], axis=1).astype(bf)
            low = dot(to_rows[g], packed).astype(bf)
            dqkv[hd, PAD * g : PAD * g + PAD, :] = low
            sums = jnp.concatenate(
                [
                    jnp.sum(low[:, 0:HD].astype(f32), axis=0, keepdims=True),
                    jnp.sum(mine.astype(f32), axis=0, keepdims=True),
                ],
                axis=1,
            )
            time_sums.append(jnp.broadcast_to(sums, (16, 2 * HD)))
        sums = jnp.concatenate(time_sums, axis=0)
        sums = jnp.where(lax.broadcasted_iota(jnp.int32, (32, 1), 0) % 16 == 0, sums, 0.0)
        high = sums.astype(bf)
        rest = (sums - high.astype(f32)).astype(bf)
        tsum[hd, 0] = high
        tsum[hd, 1] = rest
        return carry

    def rows_backward(hd, carry):
        w_head = wa[hd].reshape(D, HALF)
        for g in (0, 1):
            totals[g] += dot_nt(dqkv[hd, PAD * g : PAD * g + PAD], w_head[:, 0:256])
        return carry

    def weights_backward(hd, carry):
        grad_t = dot_tn(time_rows, tsum[hd, 0]) + dot_tn(time_rows, tsum[hd, 1])
        grad_qkv = dot_tn(f_a[...], dqkv[hd])
        grad_o = dot_tn(f_g[...], mixed[hd])
        packed = jnp.concatenate(
            [grad_qkv[:, 0:LANE_O], grad_o, grad_t, jnp.zeros((D, LANE_E - LANE_P), f32)], axis=1
        )
        wa[hd, :, :, :, 0:LANE_E] = packed.astype(bf).reshape(4, 2, UNIT, LANE_E)
        return carry

    out_ref[...] = (out_ref[...] + mlp_sum.end() + par[5]) * valid
    totals[...] = jnp.zeros_like(totals)
    lax.fori_loop(0, 2, head_backward, 0)
    sc_m.second()
    lax.fori_loop(2, 4, head_backward, 0)
    sc_m.third()
    for steps in x_steps + z_steps:
        signal(credit, steps)
    lax.fori_loop(0, 4, rows_backward, 0)
    attn_grad = Sums(totals.at[c], cut_sib, cut_yh, got_sib, got_yh)
    cut_sib[...] = totals[1 - c].astype(bf)
    attn_grad.sib.start()
    lax.fori_loop(0, 4, weights_backward, 0)
    sc_a = Scatter(wa, fin_a, got_yl.at[1])
    pl.semaphore_wait(credit, 6)
    sc_a.first()
    attn_grad.pass_on()

    def fold(hd, carry):
        for i in range(SIDE):
            off = SIDE * (SIDE - 1 - i)
            small[hd, 0:SIDE, off : off + CELLS] += bias[hd, SIDE * i : SIDE * i + SIDE, :]
        return carry

    lax.fori_loop(0, 4, fold, 0)
    small_x = [
        wire.copy(small.at[lax.rem(x + s, 4)], strips.at[s - 1], x=s) for s in (1, 2, 3)
    ]
    start(small_x)
    sc_m.fourth()

    unit_a, rstd_a = normalised(tok_ref[...])
    gy = attn_grad.end()
    rgrad[0:1] = jnp.sum(gy * unit_a, axis=0, keepdims=True)
    rgrad[1:2] = jnp.sum(gy, axis=0, keepdims=True)
    rg_x = [wire.copy(rgrad, got_rg.at[s - 1], x=s) for s in (1, 2, 3)]
    start(rg_x)
    gtok_ref[...] = gtok_ref[...] + norm_back(gy, par[0], unit_a, rstd_a)

    recv(small_x)
    drain(small_x)
    small[x] = small[x] + strips[0] + strips[1] + strips[2]
    small_z = [wire.copy(small.at[x], got_small.at[s - 1], z=s) for s in (1, 2, 3)]
    start(small_z)
    recv(rg_x)
    drain(rg_x)
    rgrad[...] = rgrad[...] + got_rg[0] + got_rg[1] + got_rg[2]
    rg_z = [wire.copy(rgrad, got_rg.at[s + 2], z=s) for s in (1, 2, 3)]
    start(rg_z)
    sc_m.end()
    sc_a.second()
    recv(small_z)
    drain(small_z)
    small[x] = small[x] + got_small[0] + got_small[1] + got_small[2]
    small_y = wire.copy(small.at[x], got_small.at[3], yl=1)
    small_y.start()
    recv(rg_z)
    drain(rg_z)
    rgrad[...] = rgrad[...] + got_rg[3] + got_rg[4] + got_rg[5]
    rg_y = [wire.copy(rgrad, got_rg7.at[k], **s) for k, s in enumerate(y_steps)]
    start(rg_y)
    sc_a.third()
    small_y.wait_recv()
    small_y.wait_send()
    fin_small[c] = small[x] + got_small[3]
    small_c = wire.copy(fin_small.at[c], fin_small.at[c], c=1)
    small_c.start()
    recv(rg_y)
    drain(rg_y)
    total = rgrad[...]
    for k in range(7):
        total = total + got_rg7[k]
    fin_rows[...] = total
    sc_a.fourth()
    sc_a.end()
    small_c.wait_recv()
    drain([small_c, info_copy])


def strip_of(table):
    t = table.reshape(39, 39)[::-1, ::-1]
    return jnp.stack([t[:, 19 - j : 39 - j] for j in range(SIDE)], axis=0).reshape(SIDE, 780)


def table_of(strip):
    s = strip.reshape(-1, SIDE, 39, SIDE)
    t = sum(jnp.pad(s[:, j], ((0, 0), (0, 0), (19 - j, j))) for j in range(SIDE))
    return t[:, ::-1, ::-1].reshape(-1, 1521)


def body(
    tokens,
    cotangent,
    time_embed,
    attend_weight,
    time_weight,
    out_weight,
    expand_weight,
    reduce_weight,
    row_params,
    expand_bias,
    bias_table,
    grid_height,
    grid_width,
    group_count,
    group_bucket,
    shares,
):
    c, x = lax.axis_index("c"), lax.axis_index("x")
    time_row = lax.dynamic_index_in_dim(time_embed, group_bucket[0], 0, keepdims=False)
    share_f = shares.astype(f32)
    weight = share_f[lax.axis_index(DP)] * share_f.shape[0] / jnp.sum(share_f)
    here = jnp.stack(
        [
            grid_height[x].astype(f32),
            grid_width[x].astype(f32),
            (x < group_count[0]).astype(f32),
            weight,
        ]
    )
    scal = jnp.zeros((8, 128), f32).at[0, 0:4].set(here)
    info = jnp.zeros((16, D), f32).at[0].set(time_row).at[1, 0:3].set(here[0:3]).astype(bf)
    strip = jnp.zeros((32, STRIP), f32)
    strip = strip.at[0:SIDE, 0:780].set(strip_of(lax.dynamic_index_in_dim(bias_table[0], c, 0, False)))
    strip = strip.at[24, 0:288].set(lax.dynamic_slice(expand_bias[0], (288 * c,), (288,)))

    heads = jnp.concatenate([attend_weight[0], out_weight[0].T[None], time_weight[0]], axis=0)
    heads = heads.reshape(6, HD, 2, HD).transpose(2, 1, 0, 3).reshape(2, HD, 432)
    pars = jnp.broadcast_to(row_params[0].T[None], (2, HD, 6))
    pars = jnp.pad(pars, ((0, 0), (0, 0), (0, 10)))
    hidden = [w[0].reshape(2, 288, HD).transpose(0, 2, 1) for w in (expand_weight, reduce_weight)]
    pack = jnp.concatenate([heads, pars, *hidden], axis=2)
    pack = jnp.pad(pack, ((0, 0), (0, 8), (0, 0)))

    vmem = pl.BlockSpec(memory_space=pltpu.VMEM)

    def shape(*dims, kind=bf):
        return pltpu.VMEM(dims, kind)

    scratch = [
        shape(4, 4, 2, UNIT, HALF),
        shape(4, 4, 2, UNIT, HALF),
        shape(80, HALF),
        shape(80, HALF),
        shape(2, 16, D),
        shape(4, 32, STRIP, kind=f32),
        shape(ROWS, D),
        shape(ROWS, D),
        shape(ROWS, D),
        shape(ROWS, D),
        shape(2, CELLS, PAD),
        shape(2, PAD, CELLS),
        shape(2, 1, CELLS, kind=f32),
        shape(8, CELLS, 256),
        shape(8, CELLS, CELLS),
        shape(4, CELLS, CELLS, kind=f32),
        shape(4, ROWS, HD),
        shape(4, ROWS, 256),
        shape(4, 2, 32, 2 * HD),
        shape(2, D, 576),
        shape(2, D, 576),
        shape(2, ROWS, 576),
        shape(2, ROWS, 576),
        shape(2, PAD, D, kind=f32),
        shape(PAD, D),
        shape(OWN, D),
        shape(PAD, D),
        shape(OWN, D),
        shape(PAD, D),
        shape(OWN, D),
        shape(PAD, D),
        shape(OWN, D),
        shape(3, 4, UNIT, HALF),
        shape(3, 4, UNIT, HALF),
        shape(3, UNIT, HALF),
        shape(3, UNIT, HALF),
        shape(2, UNIT, HALF),
        shape(4, 32, STRIP, kind=f32),
        shape(4, 32, STRIP, kind=f32),
        shape(8, D, kind=f32),
        shape(6, 8, D, kind=f32),
        shape(7, 8, D, kind=f32),
        pltpu.SemaphoreType.DMA((N_SEMS,)),
        pltpu.SemaphoreType.DMA((N_SEMS,)),
        pltpu.SemaphoreType.REGULAR,
        pltpu.SemaphoreType.DMA,
    ]
    out, gtok, fin_a, fin_m, fin_small, fin_rows = pl.pallas_call(
        layer_kernel,
        out_shape=(
            jax.ShapeDtypeStruct((OWN, D), f32),
            jax.ShapeDtypeStruct((OWN, D), f32),
            jax.ShapeDtypeStruct((2, UNIT, HALF), f32),
            jax.ShapeDtypeStruct((2, UNIT, HALF), f32),
            jax.ShapeDtypeStruct((2, 32, STRIP), f32),
            jax.ShapeDtypeStruct((8, D), f32),
        ),
        in_specs=[vmem] * 3 + [pl.BlockSpec(memory_space=pl.ANY)] + [vmem] * 3,
        out_specs=(vmem,) * 6,
        scratch_shapes=scratch,
        compiler_params=pltpu.CompilerParams(
            collective_id=0, has_side_effects=True, vmem_limit_bytes=63 * 2**20
        ),
    )(pack[:, :, 0:HALF], pack[:, :, HALF:], tokens, cotangent, info, scal, strip)

    fin = jnp.concatenate([fin_a, fin_m], axis=2)
    fin = lax.dynamic_slice_in_dim(fin, HD * c, HD, axis=1)
    heads = fin[:, :, 0:432].reshape(2, HD, 6, HD).transpose(2, 1, 0, 3).reshape(6, HD, 2 * HD)
    expand = fin[:, :, 448:736].transpose(0, 2, 1).reshape(576, HD)
    reduce = fin[:, :, 736:1024].transpose(0, 2, 1).reshape(576, HD)
    rows = lax.dynamic_slice_in_dim(fin_rows[0:6], HD * lax.axis_index(DP), HD, axis=1)
    return (
        out,
        gtok,
        heads[None, 0:3],
        heads[None, 4:6],
        heads[3].T[None],
        expand[None],
        reduce[None],
        rows[None],
        fin_small[:, 24, 0:288].reshape(1, 576),
        table_of(fin_small[:, 0:SIDE, 0:780])[None],
    )


def solution(mesh):
    torus = Mesh(mesh.devices.reshape(tuple(SIZES[a] for a in AXES)), AXES)
    rows = P(DP + MP, None)
    in_specs = (
        rows,
        rows,
        P(),
        P(None, None, DP, MP),
        P(None, None, DP, MP),
        P(None, MP, DP),
        P(None, MP, DP),
        P(None, MP, DP),
        P(None, None, DP),
        P(None, MP),
        P(None, MP, None),
        P(DP),
        P(DP),
        P(DP),
        P(DP),
        P(),
    )
    out_specs = (
        rows,
        rows,
        P(None, None, DP, MP),
        P(None, None, DP, MP),
        P(None, MP, DP),
        P(None, MP, DP),
        P(None, MP, DP),
        P(None, None, DP),
        P(None, MP),
        P(None, MP, None),
    )
    return jax.shard_map(body, mesh=torus, in_specs=in_specs, out_specs=out_specs, check_vma=False)
```

```python
import functools

import jax
import jax.numpy as jnp
from jax import lax
from jax.experimental import pallas as pl
from jax.experimental.pallas import tpu as pltpu
from jax.sharding import Mesh
from jax.sharding import PartitionSpec as P

AXES = ("z", "yl", "c", "x", "yh")
SIZES = {"z": 4, "yl": 2, "c": 2, "x": 4, "yh": 2}
DP = ("z", "yl", "c")
MP = ("x", "yh")

D = 1152
HD = 72
PAD = 320
OWN = 160
ROWS = 640
SIDE = 20
CELLS = 400
STRIP = 896
SCALE = 72**-0.5
EPSILON = 1e-06
MASKED = -1e30
UNIT = 144
FIRST = 256
LANE_P = 216
LANE_O = 224
SECOND = 640
LANE_R = 288
LANE_W = 576
EARLY = 512

bf = jnp.bfloat16
f32 = jnp.float32


def dot(a, b):
    return jnp.dot(a, b, preferred_element_type=f32)


def dot_nt(a, b):
    return lax.dot_general(a, b, (((1,), (1,)), ((), ())), preferred_element_type=f32)


def dot_tn(a, b):
    return lax.dot_general(a, b, (((0,), (0,)), ((), ())), preferred_element_type=f32)


def normalised(values):
    centred = values - jnp.mean(values, axis=-1, keepdims=True)
    rstd = lax.rsqrt(jnp.mean(centred * centred, axis=-1, keepdims=True) + EPSILON)
    return centred * rstd, rstd


def norm_back(grad, gain, unit, rstd):
    scaled = grad * gain
    inner = jnp.mean(scaled, axis=-1, keepdims=True)
    along = jnp.mean(scaled * unit, axis=-1, keepdims=True)
    return rstd * (scaled - inner - unit * along)


def gelu_pair(h):
    k0 = 0.7978845608028654
    k1 = 0.044715
    sq = h * h
    t = jnp.tanh(k0 * h * (1.0 + k1 * sq))
    half = 0.5 * (1.0 + t)
    slope = half + 0.5 * h * (1.0 - t * t) * (k0 * (1.0 + 3.0 * k1 * sq))
    return h * half, slope


def cell_maps(height, width, live, to_cells, to_rows, mask):
    def cells(shape, dim):
        a = lax.broadcasted_iota(jnp.int32, shape, dim)
        r = (a * 3277) >> 16
        c = a - r * SIDE
        return r.astype(f32), c.astype(f32)

    def hot(shape, cell_dim):
        r, c = cells(shape, cell_dim)
        p = lax.broadcasted_iota(jnp.int32, shape, 1 - cell_dim).astype(f32)
        hit = (r < height) & (c < width) & (live > 0.5) & (r * width + c == p)
        return jnp.where(hit, 1.0, 0.0).astype(bf)

    r, c = cells((1, CELLS), 1)
    mask[...] = jnp.where((r < height) & (c < width) & (live > 0.5), 0.0, MASKED)
    to_cells[...] = hot((CELLS, PAD), 0)
    to_rows[...] = hot((PAD, CELLS), 1)


class Wire:
    def __init__(self, sends, recvs):
        self.sends, self.recvs, self.used = sends, recvs, 0

    def copy(self, src, dst, **steps):
        at = self.used
        self.used += 1
        return pltpu.make_async_remote_copy(
            src_ref=src,
            dst_ref=dst,
            send_sem=self.sends.at[at],
            recv_sem=self.recvs.at[at],
            device_id=away(**steps),
            device_id_type=pl.DeviceIdType.MESH,
        )


def away(**steps):
    return {a: lax.rem(lax.axis_index(a) + s, SIZES[a]) for a, s in steps.items()}


def signal(semaphore, steps):
    pl.semaphore_signal(
        semaphore, inc=1, device_id=away(**steps), device_id_type=pl.DeviceIdType.MESH
    )


def start(copies):
    for one in copies:
        one.start()


def recv(copies):
    for one in copies:
        one.wait_recv()


def drain(copies):
    for one in copies:
        one.wait_send()


N_SEMS = 176


def layer_kernel(
    pack_a,
    pack_m,
    tok_ref,
    cot_ref,
    tile_in,
    time_in,
    time_w,
    strip_in,
    out_ref,
    gtok_ref,
    fin_a,
    fin_m,
    fin_small,
    fin_rows,
    fin_time,
    wa,
    wm,
    in_pack_a,
    in_pack_m,
    tiles,
    t16,
    tb_out,
    tb_in,
    tb,
    strips,
    f_a,
    f_m,
    f_c,
    f_g,
    to_cells,
    to_rows,
    masks,
    cells,
    probs,
    strip,
    bias,
    mixed,
    dqkv,
    we,
    wr,
    act,
    gh,
    totals,
    cut_sib,
    cut_yh,
    got_sib,
    got_yh,
    cut_sib2,
    cut_yh2,
    got_sib2,
    got_yh2,
    got_x4,
    got_z4,
    got_z1,
    got_x1,
    got_yl,
    small,
    got_small,
    rgrad,
    got_rg,
    got_rg7,
    tsum,
    got_ts,
    tall,
    sends,
    recvs,
    local,
):
    z, yl, c, x, yh = (lax.axis_index(a) for a in AXES)
    wire = Wire(sends, recvs)
    pair = 2 * z + yl
    own_at = pl.multiple_of((2 * c + yh) * OWN, OWN)
    yhp_at = pl.multiple_of((2 * c + 1 - yh) * OWN, OWN)
    own_rows = pl.ds(own_at, OWN)
    yhp_rows = pl.ds(yhp_at, OWN)
    other_group = pl.ds(pl.multiple_of((1 - c) * PAD, PAD), PAD)
    own_group = pl.ds(pl.multiple_of(c * PAD, PAD), PAD)
    near_half = pl.ds(pl.multiple_of(yh * OWN, OWN), OWN)
    far_half = pl.ds(pl.multiple_of((1 - yh) * OWN, OWN), OWN)
    part, part2 = totals.at[0], totals.at[1]

    x_steps = [dict(x=s) for s in (1, 2, 3)]
    z_steps = [dict(z=s) for s in (1, 2, 3)]
    y_steps = [dict(yl=a, c=b, yh=d) for a in (0, 1) for b in (0, 1) for d in (0, 1) if a + b + d]
    dp_steps = [dict(z=a, yl=b, c=d) for a in range(4) for b in (0, 1) for d in (0, 1) if a + b + d]
    barrier = pltpu.get_barrier_semaphore()
    greeted = x_steps + dp_steps + [s for s in y_steps if s["yh"]]
    for steps in greeted:
        signal(barrier, steps)
    pl.semaphore_wait(barrier, len(greeted))

    class Gather:
        def __init__(self, pack, landing, weights):
            self.pack, self.landing, self.w = pack, landing, weights
            self.sib = wire.copy(pack.at[1 - c], landing, c=1)
            own = weights.at[x, z, yl]
            self.low = wire.copy(own, own, yl=1)
            a, b = weights.at[x, z, 0], weights.at[x, z, 1]
            self.one = (
                [wire.copy(a, a, **s) for s in z_steps],
                [wire.copy(b, b, **s) for s in x_steps],
            )
            a, b = weights.at[x, :, 0], weights.at[:, z, 1]
            self.two = (
                [wire.copy(a, a, x=s) for s in (1, 3)],
                [wire.copy(b, b, z=s) for s in (1, 3)],
            )
            left, right = lax.rem(x + 3, 4), lax.rem(x + 1, 4)
            a, b = weights.at[left, 0:2, 0], weights.at[right, 2:4, 0]
            under, over = lax.rem(z + 3, 4), lax.rem(z + 1, 4)
            d, e = weights.at[0:2, under, 1], weights.at[2:4, over, 1]
            self.pass_x = [wire.copy(a, a, x=1), wire.copy(b, b, x=3)]
            self.pass_z = [wire.copy(d, d, z=1), wire.copy(e, e, z=3)]

        def unit(self):
            self.sib.wait_recv()
            mine = self.pack[c].astype(f32)
            other = self.landing[...].astype(f32)
            first = jnp.where(c == 0, mine, other)[:HD]
            second = jnp.where(c == 0, other, mine)[:HD]
            self.w[x, z, yl] = jnp.concatenate([first, second], axis=0).astype(bf)
            self.low.start()

            @pl.when(yl == 0)
            def _():
                start(self.one[0])

            @pl.when(yl == 1)
            def _():
                start(self.one[1])

        def other_unit(self):
            self.low.wait_recv()

            @pl.when(yl == 0)
            def _():
                start(self.one[1])

            @pl.when(yl == 1)
            def _():
                start(self.one[0])

        def spread(self, kind):
            recv(self.one[kind])
            start(self.two[kind])

        def forward(self):
            for k in (0, 1):
                self.two[0][k].wait_recv()
                self.pass_x[k].start()
                self.two[1][k].wait_recv()
                self.pass_z[k].start()

        def end(self):
            recv(self.pass_x + self.pass_z)
            drain([self.sib, self.low, *self.one[0], *self.one[1]])
            drain([*self.two[0], *self.two[1], *self.pass_x, *self.pass_z])

    class Rows:
        def __init__(self, full):
            own, far = full.at[own_rows], full.at[yhp_rows]
            self.yh = wire.copy(own, own, yh=1)
            self.sib = wire.copy(own, own, c=1)
            self.fwd = wire.copy(far, far, c=1)

        def start(self):
            start([self.yh, self.sib])

        def pass_on(self):
            self.yh.wait_recv()
            self.fwd.start()

        def end(self):
            recv([self.sib, self.fwd])
            drain([self.sib, self.fwd, self.yh])

    class Sums:
        def __init__(self, total, cut_s, cut_y, got_s, got_y):
            self.total, self.cut_s, self.cut_y = total, cut_s, cut_y
            self.got_s, self.got_y = got_s, got_y
            self.sib = wire.copy(cut_s, got_s, c=1)
            self.yh = wire.copy(cut_y, got_y, yh=1)

        def pass_on(self):
            self.sib.wait_recv()
            far = self.total[far_half] + self.got_s[far_half].astype(f32)
            self.cut_y[...] = far.astype(bf)
            self.yh.start()

        def end(self):
            self.yh.wait_recv()
            own = self.total[near_half] + self.got_s[near_half].astype(f32)
            drain([self.sib, self.yh])
            return own + self.got_y[...].astype(f32)

    class Scatter:
        def __init__(self, grads, final, x4, z4, z1, x1, low):
            self.g, self.final, self.low_in = grads, final, low
            self.x4, self.z4, self.z1, self.x1 = x4, z4, z1, x1
            self.one, self.pieces = [], []

        def later(self):
            g = self.g
            self.two = (
                [wire.copy(g.at[x, lax.rem(z + s, 4), 0], self.z1(s - 1), z=s) for s in (1, 2, 3)],
                [wire.copy(g.at[lax.rem(x + s, 4), z, 1], self.x1(s - 1), x=s) for s in (1, 2, 3)],
            )
            self.low = wire.copy(g.at[x, z, 1 - yl], self.low_in, yl=1)
            self.sib = wire.copy(self.final.at[c], self.final.at[c], c=1)

        def piece(self, at):
            copies = []
            for s in (1, 2, 3):
                src = self.g.at[lax.rem(x + s, 4), :, 0, :, at]
                copies.append(wire.copy(src, self.x4(s - 1).at[:, :, at], x=s))
                src = self.g.at[:, lax.rem(z + s, 4), 1, :, at]
                copies.append(wire.copy(src, self.z4(s - 1).at[:, :, at], z=s))
            self.one += copies
            return copies

        def second(self):
            recv(self.one)

            def add(k, carry):
                total = self.g[x, k, 0].astype(f32)
                for s in range(3):
                    total = total + self.x4(s)[k].astype(f32)
                self.g[x, k, 0] = total.astype(bf)
                total = self.g[k, z, 1].astype(f32)
                for s in range(3):
                    total = total + self.z4(s)[k].astype(f32)
                self.g[k, z, 1] = total.astype(bf)
                return carry

            lax.fori_loop(0, 4, add, 0)
            start(self.two[0] + self.two[1])

        def third(self):
            recv(self.two[0] + self.two[1])
            for t, got in ((0, self.z1), (1, self.x1)):
                total = self.g[x, z, t].astype(f32)
                for s in range(3):
                    total = total + got(s)[...].astype(f32)
                self.g[x, z, t] = total.astype(bf)
            self.low.start()

        def fourth(self):
            self.low.wait_recv()
            self.final[c] = self.g[x, z, yl].astype(f32) + self.low_in[...].astype(f32)
            self.sib.start()

        def end(self):
            self.sib.wait_recv()
            drain([*self.one, *self.two[0], *self.two[1], self.low, self.sib])

    w_a = Gather(pack_a, in_pack_a, wa)
    w_m = Gather(pack_m, in_pack_m, wm)
    rows_a, rows_c, rows_m, rows_g = Rows(f_a), Rows(f_c), Rows(f_m), Rows(f_g)
    here = 2 * pair + c
    tile_copies = [wire.copy(tiles.at[here], tiles.at[here], **s) for s in dp_steps]
    strip_copies = [wire.copy(strips.at[x], strips.at[x], **s) for s in x_steps]

    def there(steps):
        far_pair = 2 * lax.rem(z + steps["z"], 4) + lax.rem(yl + steps["yl"], 2)
        return far_pair, lax.rem(c + steps["c"], 2)

    tb_copies = [
        wire.copy(tb_out.at[there(s)[0], there(s)[1]], tb_in.at[k], **s)
        for k, s in enumerate(dp_steps)
    ]
    tb_x = [wire.copy(tb.at[x], tb.at[x], **s) for s in x_steps]

    w_a.sib.start()
    cot_copy = pltpu.make_async_copy(cot_ref, gtok_ref, local)
    cot_copy.start()
    tiles[here] = tile_in[...]
    start(tile_copies)
    strips[x] = strip_in[...]
    height, width, live, share = (tile_in[k : k + 1, 0:1] for k in (1, 2, 3, 4))
    w_a.unit()
    unit_a, _ = normalised(tok_ref[...])
    f_a[own_rows] = unit_a.astype(bf)
    rows_a.start()
    start(strip_copies)
    w_m.sib.start()

    by_bucket = dot(time_in[...], time_w[...])
    position = lax.broadcasted_iota(jnp.int32, (OWN, 1), 0).astype(f32)
    position = position + (yh * OWN).astype(f32)
    valid = jnp.where((position < height * width) & (live > 0.5), 1.0, 0.0)
    cot_copy.wait()
    gtok_ref[...] = gtok_ref[...] * share * valid
    f_c[own_rows] = gtok_ref[...].astype(bf)
    w_a.other_unit()

    recv(tile_copies)
    drain(tile_copies)
    bucket = jnp.concatenate([tiles[d, 0:1, 0:32] for d in range(16)], axis=0)
    is_bucket = bucket == lax.broadcasted_iota(jnp.int32, (16, 32), 1).astype(f32)
    is_bucket = jnp.where(is_bucket, 1.0, 0.0).astype(bf)
    t16[...] = dot(is_bucket, time_in[...]).astype(bf)
    high = by_bucket.astype(bf)
    rest = (by_bucket - high.astype(f32)).astype(bf)
    by_group = dot(is_bucket, high) + dot(is_bucket, rest)
    tb_out[...] = jnp.zeros_like(tb_out)
    for p in range(8):
        for k in (0, 1):
            tb_out[p, k, 0:2, 0:UNIT] = by_group[2 * p : 2 * p + 2, UNIT * k : UNIT * k + UNIT]
    start(tb_copies)
    w_a.spread(0)
    w_a.spread(1)
    w_m.unit()
    rows_a.pass_on()
    rows_c.start()
    for g in (0, 1):
        cell_maps(
            *(tiles[2 * pair + g, k : k + 1, 0:1] for k in (1, 2, 3)),
            to_cells.at[g],
            to_rows.at[g],
            masks.at[g],
        )
    recv(strip_copies)
    drain(strip_copies)

    lane = lax.broadcasted_iota(jnp.int32, (1, STRIP), 1)
    even = lane - 40 * ((lane * 1639) >> 16) < SIDE

    def build_bias(hd, carry):
        for j in range(SIDE):
            one = pltpu.roll(strips[hd, 0:1], STRIP - (19 - j), axis=1)
            two = pltpu.roll(strips[hd, 1:2], (STRIP + SIDE - (19 - j)) % STRIP, axis=1)
            strip[j : j + 1] = jnp.where(even, one, two)
        for i in range(SIDE):
            off = SIDE * (SIDE - 1 - i)
            bias[hd, SIDE * i : SIDE * i + SIDE, :] = strip[0:SIDE, off : off + CELLS]
        return carry

    lax.fori_loop(0, 2, build_bias, 0)
    w_m.other_unit()
    recv(tb_copies)
    total = tb_out[pair, c]
    for k in range(15):
        total = total + tb_in[k]
    tb[x] = total
    drain(tb_copies)
    start(tb_x)
    lax.fori_loop(2, 4, build_bias, 0)
    rows_a.end()
    w_a.forward()
    rows_c.pass_on()
    recv(tb_x)
    drain(tb_x)
    w_a.end()
    w_m.spread(0)
    w_m.spread(1)

    row_id = lax.broadcasted_iota(jnp.int32, (16, 128), 0)
    lane_id = lax.broadcasted_iota(jnp.int32, (16, 128), 1)
    pick = jnp.where(lane_id == row_id + (LANE_P - 128), 1.0, 0.0).astype(bf)
    params = dot_nt(pick, wa[0].reshape(D, FIRST)[:, 128:256])
    par = [params[k : k + 1] for k in range(6)]

    def gain_rows(i, carry):
        at = pl.ds(pl.multiple_of(i * 64, 64), 64)
        f_a[at] = (f_a[at].astype(f32) * par[0] + par[1]).astype(bf)
        return carry

    lax.fori_loop(0, ROWS // 64, gain_rows, 0)

    lanes256 = lax.broadcasted_iota(jnp.int32, (1, 256), 1)

    def head_forward(hd, carry):
        qkv = dot(f_a[...], wa[hd].reshape(D, FIRST))
        for g in (0, 1):
            time_g = tb[hd, g : g + 1]
            low = (qkv[PAD * g : PAD * g + PAD] + jnp.where(lanes256 < HD, time_g, 0.0)).astype(bf)
            cell = dot(to_cells[g], low).astype(bf)
            cells[2 * hd + g] = cell
            score = dot_nt(cell[:, 0:HD], cell[:, HD : 2 * HD]) * SCALE + bias[hd] + masks[g]
            score = jnp.exp(score - jnp.max(score, axis=-1, keepdims=True))
            prob = (score * (1.0 / jnp.sum(score, axis=-1, keepdims=True))).astype(bf)
            probs[2 * hd + g] = prob
            o = dot(to_rows[g], dot(prob, cell[:, 2 * HD : 3 * HD]).astype(bf))
            mixed[hd, PAD * g : PAD * g + PAD, :] = (o + time_g[:, HD : 2 * HD]).astype(bf)
        return carry

    lax.fori_loop(0, 2, head_forward, 0)
    rows_c.end()
    lax.fori_loop(2, 4, head_forward, 0)
    w_m.forward()
    w_m.end()

    def out_weight(hd):
        start_ = wm[hd].reshape(D, SECOND)[:, LANE_W:SECOND]
        return jnp.concatenate([start_, wa[hd].reshape(D, FIRST)[:, LANE_O : LANE_O + 8]], axis=1)

    def out_project(at):
        total = jnp.zeros((PAD, D), f32)
        for hd in range(4):
            total = total + dot_nt(mixed[hd, at], out_weight(hd))
        return total

    attn_sum = Sums(part, cut_sib, cut_yh, got_sib, got_yh)
    cut_sib[...] = out_project(other_group).astype(bf)
    attn_sum.sib.start()
    part[...] = out_project(own_group)
    attn_sum.pass_on()

    for hd in range(4):
        p, at = hd // 2, 288 * (hd % 2)
        both = wm[hd].reshape(D, SECOND)
        we[p, :, :, at : at + 288] = both[:, 0:288].reshape(8, UNIT, 288)
        wr[p, :, at : at + 288] = both[:, LANE_R : LANE_R + 288]
    out_ref[...] = tok_ref[...] + par[2] + attn_sum.end()
    unit_m, _ = normalised(out_ref[...])
    f_m[own_rows] = (unit_m * par[3] + par[4]).astype(bf)
    rows_m.start()
    rows_m.pass_on()
    rows_m.end()

    def mlp(at):
        total = jnp.zeros((PAD, D), f32)
        for p in (0, 1):
            hidden_bias = jnp.concatenate([strips[2 * p + k, 2:3, 0:288] for k in (0, 1)], axis=1)
            w_e = we[p].reshape(D, 576)
            value, slope = gelu_pair(dot(f_m[at], w_e) + hidden_bias)
            act[p, at] = value.astype(bf)
            low = (dot(f_c[at], wr[p]) * slope).astype(bf)
            gh[p, at] = low
            total = total + dot_nt(low, w_e)
        return total

    mlp_grad = Sums(part, cut_sib, cut_yh, got_sib, got_yh)
    cut_sib[...] = mlp(other_group).astype(bf)
    mlp_grad.sib.start()
    part[...] = mlp(own_group)
    mlp_grad.pass_on()

    def mlp_out(at):
        return dot_nt(act[0, at], wr[0]) + dot_nt(act[1, at], wr[1])

    mlp_sum = Sums(part2, cut_sib2, cut_yh2, got_sib2, got_yh2)
    cut_sib2[...] = mlp_out(other_group).astype(bf)
    mlp_sum.sib.start()
    part2[...] = mlp_out(own_group)

    sc_m = Scatter(
        wm,
        fin_m,
        lambda s: got_x4.at[s],
        lambda s: got_z4.at[s],
        lambda s: got_z1.at[s],
        lambda s: got_x1.at[s],
        got_yl,
    )
    early = sc_m.piece(pl.ds(0, EARLY))
    late = sc_m.piece(pl.ds(EARLY, SECOND - EARLY))
    sc_m.later()
    small[...] = jnp.zeros_like(small)
    ones = jnp.ones((16, ROWS), bf)
    for p in (0, 1):
        bias_sum = dot(ones, gh[p])
        grad_e = dot_tn(f_m[...], gh[p]).astype(bf).reshape(4, 2, UNIT, 576)
        for k in (0, 1):
            hd, at = 2 * p + k, 288 * k
            small[hd, 2:3, 0:288] = bias_sum[0:1, at : at + 288]
            wm[hd, :, :, :, 0:288] = grad_e[:, :, :, at : at + 288]
        grad_r = dot_tn(f_c[...], act[p]).astype(bf).reshape(4, 2, UNIT, 576)
        for k in (0, 1):
            hd, at = 2 * p + k, 288 * k
            wm[hd, :, :, :, LANE_R : LANE_R + 288] = grad_r[:, :, :, at : at + 288]
    start(early)

    unit_m, rstd_m = normalised(out_ref[...])
    gy = mlp_grad.end()
    rgrad[...] = jnp.zeros_like(rgrad)
    rgrad[3:4] = jnp.sum(gy * unit_m, axis=0, keepdims=True)
    rgrad[4:5] = jnp.sum(gy, axis=0, keepdims=True)
    rgrad[5:6] = jnp.sum(f_c[own_rows].astype(f32), axis=0, keepdims=True)
    gtok_ref[...] = gtok_ref[...] + norm_back(gy, par[3], unit_m, rstd_m)
    low_mid = gtok_ref[...].astype(bf)
    rgrad[2:3] = jnp.sum(low_mid.astype(f32), axis=0, keepdims=True)
    f_g[own_rows] = low_mid
    rows_g.start()
    mlp_sum.pass_on()
    rows_g.pass_on()
    bias[...] = jnp.zeros_like(bias)
    rows_g.end()

    def mixed_backward(hd, carry):
        dqkv[hd, :, 0:HD] = dot(f_g[...], out_weight(hd)).astype(bf)
        grad_o = dot_tn(f_g[...], mixed[hd]).astype(bf).reshape(4, 2, UNIT, HD)
        wm[hd, :, :, :, LANE_W:SECOND] = grad_o[:, :, :, 0:64]
        wa[hd, :, :, :, LANE_O : LANE_O + 8] = grad_o[:, :, :, 64:HD]
        return carry

    lax.fori_loop(0, 4, mixed_backward, 0)
    start(late)

    def head_backward(hd, carry):
        for g in (0, 1):
            mine = dqkv[hd, PAD * g : PAD * g + PAD, 0:HD]
            dcell = dot(to_cells[g], mine).astype(bf)
            cell = cells[2 * hd + g]
            prob = probs[2 * hd + g]
            wide = prob.astype(f32)
            dprob = dot_nt(dcell, cell[:, 2 * HD : 3 * HD])
            ds = (wide * (dprob - jnp.sum(dprob * wide, axis=-1, keepdims=True))).astype(bf)
            bias[hd] += ds.astype(f32)
            dq = dot(ds, cell[:, HD : 2 * HD]) * SCALE
            dk = dot_tn(ds, cell[:, 0:HD]) * SCALE
            dv = dot_tn(prob, dcell)
            packed = jnp.concatenate([dq, dk, dv, jnp.zeros((CELLS, 40), f32)], axis=1).astype(bf)
            low = dot(to_rows[g], packed).astype(bf)
            dqkv[hd, PAD * g : PAD * g + PAD, :] = low
            tsum[hd, g : g + 1, 0:HD] = jnp.sum(low[:, 0:HD].astype(f32), axis=0, keepdims=True)
            tsum[hd, g : g + 1, HD : 2 * HD] = jnp.sum(mine.astype(f32), axis=0, keepdims=True)
        return carry

    def rows_backward(hd, carry):
        w_head = wa[hd].reshape(D, FIRST)
        for g in (0, 1):
            totals[g] += dot_nt(dqkv[hd, PAD * g : PAD * g + PAD], w_head)
        return carry

    def weights_backward(hd):
        grad_qkv = dot_tn(f_a[...], dqkv[hd]).astype(bf).reshape(4, 2, UNIT, FIRST)
        wa[hd, :, :, :, 0:LANE_P] = grad_qkv[:, :, :, 0:LANE_P]

    tsum[...] = jnp.zeros_like(tsum)
    lax.fori_loop(0, 2, head_backward, 0)
    out_ref[...] = (out_ref[...] + mlp_sum.end() + par[5]) * valid
    totals[...] = jnp.zeros_like(totals)
    sc_m.second()
    lax.fori_loop(2, 4, head_backward, 0)

    ts_x = [wire.copy(tsum.at[lax.rem(x + s, 4)], got_ts.at[s - 1], x=s) for s in (1, 2, 3)]
    start(ts_x)

    def fold(hd, carry):
        strip[...] = jnp.zeros_like(strip)
        for i in range(SIDE):
            off = SIDE * (SIDE - 1 - i)
            strip[0:SIDE, off : off + CELLS] += bias[hd, SIDE * i : SIDE * i + SIDE, :]
        one = jnp.zeros((1, STRIP), f32)
        two = jnp.zeros((1, STRIP), f32)
        for j in range(SIDE):
            row = strip[j : j + 1]
            one = one + pltpu.roll(jnp.where(even, row, 0.0), 19 - j, axis=1) if j < 19 else (
                one + jnp.where(even, row, 0.0)
            )
            shift = (STRIP + 19 - j - SIDE) % STRIP
            two = two + pltpu.roll(jnp.where(even, 0.0, row), shift, axis=1)
        small[hd, 0:1] = one
        small[hd, 1:2] = two
        return carry

    lax.fori_loop(0, 4, rows_backward, 0)
    attn_grad = Sums(totals.at[c], cut_sib, cut_yh, got_sib, got_yh)
    cut_sib[...] = totals[1 - c].astype(bf)
    attn_grad.sib.start()

    def lot(p, at, low):
        return we.at[p, pl.ds(at, 4), :, pl.ds(low, FIRST)]

    x4 = [lot(0, 0, 0), lot(0, 4, 0), lot(0, 0, FIRST)]
    z4 = [lot(0, 4, FIRST), lot(1, 0, 0), lot(1, 4, 0)]
    sc_a = Scatter(
        wa,
        fin_a,
        lambda s: x4[s],
        lambda s: z4[s],
        lambda s: we.at[1, s, :, pl.ds(FIRST, FIRST)],
        lambda s: we.at[1, s + 3, :, pl.ds(FIRST, FIRST)],
        we.at[1, 6, :, pl.ds(FIRST, FIRST)],
    )
    to_x = [wire.copy(wa.at[lax.rem(x + s, 4), :, 0], x4[s - 1], x=s) for s in (1, 2, 3)]
    sc_a.one += to_x
    for hd in range(4):
        weights_backward(hd)
        for s in (1, 2, 3):
            pl.when(lax.rem(x + s, 4) == hd)(to_x[s - 1].start)
        to_z = [
            wire.copy(wa.at[hd, lax.rem(z + s, 4), 1], z4[s - 1].at[hd], z=s) for s in (1, 2, 3)
        ]
        start(to_z)
        sc_a.one += to_z
        if hd == 0:
            sc_m.third()
        if hd == 1:
            attn_grad.pass_on()
    sc_a.later()
    lax.fori_loop(0, 4, fold, 0)
    small_x = [
        wire.copy(small.at[lax.rem(x + s, 4)], got_small.at[s - 1], x=s) for s in (1, 2, 3)
    ]
    start(small_x)
    sc_m.fourth()

    recv(ts_x)
    drain(ts_x)
    tall[here] = tsum[x] + got_ts[0] + got_ts[1] + got_ts[2]
    tall_copies = [wire.copy(tall.at[here], tall.at[here], **s) for s in dp_steps]
    start(tall_copies)
    unit_a, rstd_a = normalised(tok_ref[...])
    gy = attn_grad.end()
    rgrad[0:1] = jnp.sum(gy * unit_a, axis=0, keepdims=True)
    rgrad[1:2] = jnp.sum(gy, axis=0, keepdims=True)
    rg_x = [wire.copy(rgrad, got_rg.at[s - 1], x=s) for s in (1, 2, 3)]
    start(rg_x)
    gtok_ref[...] = gtok_ref[...] + norm_back(gy, par[0], unit_a, rstd_a)

    sc_a.second()
    recv(small_x)
    drain(small_x)
    small[x] = small[x] + got_small[0] + got_small[1] + got_small[2]
    small_z = [wire.copy(small.at[x], got_small.at[s + 2], z=s) for s in (1, 2, 3)]
    start(small_z)
    recv(rg_x)
    drain(rg_x)
    rgrad[...] = rgrad[...] + got_rg[0] + got_rg[1] + got_rg[2]
    rg_z = [wire.copy(rgrad, got_rg.at[s + 2], z=s) for s in (1, 2, 3)]
    start(rg_z)
    sc_m.end()
    recv(tall_copies)
    drain(tall_copies)
    for k in (0, 1):
        sums = jnp.concatenate([tall[2 * p + k, 0:2] for p in range(8)], axis=0)
        high = sums.astype(bf)
        rest = (sums - high.astype(f32)).astype(bf)
        grad_t = dot_tn(t16[...], high) + dot_tn(t16[...], rest)
        fin_time[0, :, HD * k : HD * k + HD] = grad_t[:, 0:HD]
        fin_time[1, :, HD * k : HD * k + HD] = grad_t[:, HD : 2 * HD]
    sc_a.third()
    recv(small_z)
    drain(small_z)
    small[x] = small[x] + got_small[3] + got_small[4] + got_small[5]
    small_y = wire.copy(small.at[x], got_small.at[6], yl=1)
    small_y.start()
    recv(rg_z)
    drain(rg_z)
    rgrad[...] = rgrad[...] + got_rg[3] + got_rg[4] + got_rg[5]
    rg_y = [wire.copy(rgrad, got_rg7.at[k], **s) for k, s in enumerate(y_steps)]
    start(rg_y)
    sc_a.fourth()
    small_y.wait_recv()
    small_y.wait_send()
    fin_small[c] = small[x] + got_small[6]
    small_c = wire.copy(fin_small.at[c], fin_small.at[c], c=1)
    small_c.start()
    recv(rg_y)
    drain(rg_y)
    total = rgrad[...]
    for k in range(7):
        total = total + got_rg7[k]
    fin_rows[...] = total
    sc_a.end()
    small_c.wait_recv()
    drain([small_c])


def strips_of(table):
    t = jnp.pad(table.reshape(39, 39)[::-1, ::-1], ((0, 1), (0, 1)))
    return t.reshape(20, 2, 40).transpose(1, 0, 2).reshape(2, 800)


def table_of(strips):
    t = strips.reshape(-1, 2, 20, 40).transpose(0, 2, 1, 3).reshape(-1, 40, 40)
    return t[:, 38::-1, 38::-1].reshape(-1, 1521)


def body(
    tokens,
    cotangent,
    time_embed,
    attend_weight,
    time_weight,
    out_weight,
    expand_weight,
    reduce_weight,
    row_params,
    expand_bias,
    bias_table,
    grid_height,
    grid_width,
    group_count,
    group_bucket,
    shares,
):
    c, x = lax.axis_index("c"), lax.axis_index("x")
    share_f = shares.astype(f32)
    place = lax.axis_index(DP)
    weight = share_f[place] * share_f.shape[0] / jnp.sum(share_f)
    here = jnp.stack(
        [
            group_bucket[0].astype(f32),
            grid_height[x].astype(f32),
            grid_width[x].astype(f32),
            (x < group_count[0]).astype(f32),
            weight,
        ]
    )
    tile = jnp.broadcast_to(jnp.pad(here, (0, 3))[:, None], (8, 128))
    strip = jnp.zeros((8, STRIP), f32)
    strip = strip.at[0:2, 0:800].set(strips_of(lax.dynamic_index_in_dim(bias_table[0], c, 0, False)))
    strip = strip.at[2, 0:288].set(lax.dynamic_slice(expand_bias[0], (288 * c,), (288,)))
    time_slice = lax.dynamic_slice_in_dim(time_embed, HD * place, HD, axis=1).astype(bf)
    time_pack = time_weight[0].reshape(2, HD, 2, HD).transpose(1, 2, 0, 3).reshape(HD, 288)

    heads = attend_weight[0].reshape(3, HD, 2, HD).transpose(2, 1, 0, 3).reshape(2, HD, 216)
    pars = jnp.broadcast_to(row_params[0].T[None], (2, HD, 6))
    outs = out_weight[0].reshape(2, HD, HD).transpose(0, 2, 1)
    hidden = [w[0].reshape(2, 288, HD).transpose(0, 2, 1) for w in (expand_weight, reduce_weight)]
    none = jnp.zeros((2, HD, 24), bf)
    pack_a = jnp.concatenate([heads, pars, none[:, :, 0:2], outs[:, :, 64:], none], axis=2)
    pack_m = jnp.concatenate([*hidden, outs[:, :, 0:64]], axis=2)
    pack_a, pack_m = (jnp.pad(p, ((0, 0), (0, 8), (0, 0))) for p in (pack_a, pack_m))

    vmem = pl.BlockSpec(memory_space=pltpu.VMEM)

    def shape(*dims, kind=bf):
        return pltpu.VMEM(dims, kind)

    scratch = [
        shape(4, 4, 2, UNIT, FIRST),
        shape(4, 4, 2, UNIT, SECOND),
        shape(80, FIRST),
        shape(80, SECOND),
        shape(16, 8, 128, kind=f32),
        shape(16, HD),
        shape(8, 2, 8, 256, kind=f32),
        shape(15, 8, 256, kind=f32),
        shape(4, 8, 256, kind=f32),
        shape(4, 8, STRIP, kind=f32),
        shape(ROWS, D),
        shape(ROWS, D),
        shape(ROWS, D),
        shape(ROWS, D),
        shape(2, CELLS, PAD),
        shape(2, PAD, CELLS),
        shape(2, 1, CELLS, kind=f32),
        shape(8, CELLS, 256),
        shape(8, CELLS, CELLS),
        shape(24, STRIP, kind=f32),
        shape(4, CELLS, CELLS, kind=f32),
        shape(4, ROWS, HD),
        shape(4, ROWS, 256),
        shape(2, 8, UNIT, 576),
        shape(2, D, 576),
        shape(2, ROWS, 576),
        shape(2, ROWS, 576),
        shape(2, PAD, D, kind=f32),
        shape(PAD, D),
        shape(OWN, D),
        shape(PAD, D),
        shape(OWN, D),
        shape(PAD, D),
        shape(OWN, D),
        shape(PAD, D),
        shape(OWN, D),
        shape(3, 4, UNIT, SECOND),
        shape(3, 4, UNIT, SECOND),
        shape(3, UNIT, SECOND),
        shape(3, UNIT, SECOND),
        shape(UNIT, SECOND),
        shape(4, 8, STRIP, kind=f32),
        shape(7, 8, STRIP, kind=f32),
        shape(8, D, kind=f32),
        shape(6, 8, D, kind=f32),
        shape(7, 8, D, kind=f32),
        shape(4, 8, 256, kind=f32),
        shape(3, 8, 256, kind=f32),
        shape(16, 8, 256, kind=f32),
        pltpu.SemaphoreType.DMA((N_SEMS,)),
        pltpu.SemaphoreType.DMA((N_SEMS,)),
        pltpu.SemaphoreType.DMA,
    ]
    out, gtok, fin_a, fin_m, fin_small, fin_rows, fin_time = pl.pallas_call(
        layer_kernel,
        out_shape=(
            jax.ShapeDtypeStruct((OWN, D), f32),
            jax.ShapeDtypeStruct((OWN, D), f32),
            jax.ShapeDtypeStruct((2, UNIT, FIRST), f32),
            jax.ShapeDtypeStruct((2, UNIT, SECOND), f32),
            jax.ShapeDtypeStruct((2, 8, STRIP), f32),
            jax.ShapeDtypeStruct((8, D), f32),
            jax.ShapeDtypeStruct((2, HD, 2 * HD), f32),
        ),
        in_specs=[vmem] * 3 + [pl.BlockSpec(memory_space=pl.ANY)] + [vmem] * 4,
        out_specs=(vmem,) * 7,
        scratch_shapes=scratch,
        compiler_params=pltpu.CompilerParams(
            collective_id=0, has_side_effects=True, vmem_limit_bytes=63 * 2**20
        ),
    )(pack_a, pack_m, tokens, cotangent, tile, time_slice, time_pack, strip)

    fin_a, fin_m = (lax.dynamic_slice_in_dim(f, HD * c, HD, axis=1) for f in (fin_a, fin_m))
    attend = fin_a[:, :, 0:216].reshape(2, HD, 3, HD).transpose(2, 1, 0, 3).reshape(3, HD, 2 * HD)
    outs = jnp.concatenate([fin_m[:, :, 576:640], fin_a[:, :, 224:232]], axis=2)
    outs = outs.transpose(0, 2, 1).reshape(2 * HD, HD)
    expand = fin_m[:, :, 0:288].transpose(0, 2, 1).reshape(576, HD)
    reduce = fin_m[:, :, 288:576].transpose(0, 2, 1).reshape(576, HD)
    rows = lax.dynamic_slice_in_dim(fin_rows[0:6], HD * place, HD, axis=1)
    return (
        out,
        gtok,
        attend[None],
        fin_time[None],
        outs[None],
        expand[None],
        reduce[None],
        rows[None],
        fin_small[:, 2, 0:288].reshape(1, 576),
        table_of(fin_small[:, 0:2, 0:800])[None],
    )


def solution(mesh):
    torus = Mesh(mesh.devices.reshape(tuple(SIZES[a] for a in AXES)), AXES)
    rows = P(DP + MP, None)
    in_specs = (
        rows,
        rows,
        P(),
        P(None, None, DP, MP),
        P(None, None, DP, MP),
        P(None, MP, DP),
        P(None, MP, DP),
        P(None, MP, DP),
        P(None, None, DP),
        P(None, MP),
        P(None, MP, None),
        P(DP),
        P(DP),
        P(DP),
        P(DP),
        P(),
    )
    out_specs = (
        rows,
        rows,
        P(None, None, DP, MP),
        P(None, None, DP, MP),
        P(None, MP, DP),
        P(None, MP, DP),
        P(None, MP, DP),
        P(None, None, DP),
        P(None, MP),
        P(None, MP, None),
    )
    return jax.shard_map(body, mesh=torus, in_specs=in_specs, out_specs=out_specs, check_vma=False)
```

```python
import functools

import jax
import jax.numpy as jnp
from jax import lax
from jax.experimental import pallas as pl
from jax.experimental.pallas import tpu as pltpu
from jax.sharding import Mesh
from jax.sharding import PartitionSpec as P

AXES = ("z", "yl", "c", "x", "yh")
SIZES = {"z": 4, "yl": 2, "c": 2, "x": 4, "yh": 2}
DP = ("z", "yl", "c")
MP = ("x", "yh")

D = 1152
HD = 72
PAD = 320
OWN = 160
ROWS = 640
SIDE = 20
CELLS = 400
STRIP = 896
SCALE = 72**-0.5
EPSILON = 1e-06
MASKED = -1e30
UNIT = 144
FIRST = 256
LANE_P = 216
LANE_O = 224
SECOND = 640
LANE_R = 288
LANE_W = 576
EARLY = 512

bf = jnp.bfloat16
f32 = jnp.float32


def dot(a, b):
    return jnp.dot(a, b, preferred_element_type=f32)


def dot_nt(a, b):
    return lax.dot_general(a, b, (((1,), (1,)), ((), ())), preferred_element_type=f32)


def dot_tn(a, b):
    return lax.dot_general(a, b, (((0,), (0,)), ((), ())), preferred_element_type=f32)


def normalised(values):
    centred = values - jnp.mean(values, axis=-1, keepdims=True)
    rstd = lax.rsqrt(jnp.mean(centred * centred, axis=-1, keepdims=True) + EPSILON)
    return centred * rstd, rstd


def norm_back(grad, gain, unit, rstd):
    scaled = grad * gain
    inner = jnp.mean(scaled, axis=-1, keepdims=True)
    along = jnp.mean(scaled * unit, axis=-1, keepdims=True)
    return rstd * (scaled - inner - unit * along)


def gelu_pair(h):
    k0 = 0.7978845608028654
    k1 = 0.044715
    sq = h * h
    t = jnp.tanh(k0 * h * (1.0 + k1 * sq))
    half = 0.5 * (1.0 + t)
    slope = half + 0.5 * h * (1.0 - t * t) * (k0 * (1.0 + 3.0 * k1 * sq))
    return h * half, slope


def cell_maps(height, width, live, to_cells, to_rows, mask):
    def cells(shape, dim):
        a = lax.broadcasted_iota(jnp.int32, shape, dim)
        r = (a * 3277) >> 16
        c = a - r * SIDE
        return (SIDE - 1 - r).astype(f32), (SIDE - 1 - c).astype(f32)

    def hot(shape, cell_dim):
        r, c = cells(shape, cell_dim)
        p = lax.broadcasted_iota(jnp.int32, shape, 1 - cell_dim).astype(f32)
        hit = (r < height) & (c < width) & (live > 0.5) & (r * width + c == p)
        return jnp.where(hit, 1.0, 0.0).astype(bf)

    r, c = cells((1, CELLS), 1)
    mask[...] = jnp.where((r < height) & (c < width) & (live > 0.5), 0.0, MASKED)
    to_cells[...] = hot((CELLS, PAD), 0)
    to_rows[...] = hot((PAD, CELLS), 1)


class Wire:
    def __init__(self, sends, recvs):
        self.sends, self.recvs, self.used = sends, recvs, 0

    def copy(self, src, dst, **steps):
        at = self.used
        self.used += 1
        return pltpu.make_async_remote_copy(
            src_ref=src,
            dst_ref=dst,
            send_sem=self.sends.at[at],
            recv_sem=self.recvs.at[at],
            device_id=away(**steps),
            device_id_type=pl.DeviceIdType.MESH,
        )


def away(**steps):
    return {a: lax.rem(lax.axis_index(a) + s, SIZES[a]) for a, s in steps.items()}


def signal(semaphore, steps):
    pl.semaphore_signal(
        semaphore, inc=1, device_id=away(**steps), device_id_type=pl.DeviceIdType.MESH
    )


def start(copies):
    for one in copies:
        one.start()


def recv(copies):
    for one in copies:
        one.wait_recv()


def drain(copies):
    for one in copies:
        one.wait_send()


N_SEMS = 176


def layer_kernel(
    gh_ref,
    gw_ref,
    gc_ref,
    gb_ref,
    sh_ref,
    tok_ref,
    cot_ref,
    te_ref,
    att_ref,
    tw_ref,
    ow_ref,
    ex_ref,
    rd_ref,
    rp_ref,
    eb_ref,
    bt_ref,
    out_ref,
    gtok_ref,
    g_att,
    g_time,
    g_out,
    g_exp,
    g_red,
    g_rows,
    g_eb,
    g_tab,
    pack_a,
    pack_m,
    fin_a,
    fin_m,
    fin_small,
    wa,
    wm,
    in_pack_a,
    in_pack_m,
    tiles,
    t16,
    tb_out,
    tb_in,
    tb,
    strips,
    f_a,
    f_m,
    f_c,
    f_g,
    to_cells,
    to_rows,
    masks,
    cells,
    probs,
    strip,
    bias,
    mixed,
    mixed_all,
    wo,
    dqkv,
    we,
    wr,
    act,
    gh,
    totals,
    cut_sib,
    cut_yh,
    got_sib,
    got_yh,
    cut_sib2,
    cut_yh2,
    got_sib2,
    got_yh2,
    got_x4,
    got_z4,
    got_z1,
    got_x1,
    got_yl,
    small,
    got_small,
    rgrad,
    got_rg,
    got_rg7,
    tsum,
    got_ts,
    tall,
    sends,
    recvs,
    local,
):
    z, yl, c, x, yh = (lax.axis_index(a) for a in AXES)
    wire = Wire(sends, recvs)
    pair = 2 * z + yl
    own_at = pl.multiple_of((2 * c + yh) * OWN, OWN)
    yhp_at = pl.multiple_of((2 * c + 1 - yh) * OWN, OWN)
    own_rows = pl.ds(own_at, OWN)
    yhp_rows = pl.ds(yhp_at, OWN)
    other_group = pl.ds(pl.multiple_of((1 - c) * PAD, PAD), PAD)
    own_group = pl.ds(pl.multiple_of(c * PAD, PAD), PAD)
    near_half = pl.ds(pl.multiple_of(yh * OWN, OWN), OWN)
    far_half = pl.ds(pl.multiple_of((1 - yh) * OWN, OWN), OWN)
    part, part2 = totals.at[0], totals.at[1]
    place = 4 * z + 2 * yl + c

    eye = lax.broadcasted_iota(jnp.int32, (80, HD), 0) == lax.broadcasted_iota(jnp.int32, (80, HD), 1)
    eye = jnp.where(eye, 1.0, 0.0).astype(bf)
    for k in (0, 1):
        pieces = [att_ref[i][:, HD * k : HD * k + HD].astype(f32) for i in range(3)]
        pieces = [jnp.concatenate([p, jnp.zeros((8, HD), f32)], axis=0) for p in pieces]
        pieces.append(dot_nt(eye, rp_ref[...]))
        pieces.append(jnp.zeros((80, 2), f32))
        pieces.append(dot_nt(eye, ow_ref[HD * k + 64 : HD * k + HD]))
        pieces.append(jnp.zeros((80, 24), f32))
        pack_a[k] = jnp.concatenate(pieces, axis=1).astype(bf)
        pieces = [w[:, 288 * k : 288 * k + 288].astype(f32) for w in (ex_ref, rd_ref)]
        pieces = [jnp.concatenate([p, jnp.zeros((8, 288), f32)], axis=0) for p in pieces]
        pieces.append(dot_nt(eye, ow_ref[HD * k : HD * k + 64]))
        pack_m[k] = jnp.concatenate(pieces, axis=1).astype(bf)

    x_steps = [dict(x=s) for s in (1, 2, 3)]
    z_steps = [dict(z=s) for s in (1, 2, 3)]
    y_steps = [dict(yl=a, c=b, yh=d) for a in (0, 1) for b in (0, 1) for d in (0, 1) if a + b + d]
    dp_steps = [dict(z=a, yl=b, c=d) for a in range(4) for b in (0, 1) for d in (0, 1) if a + b + d]
    barrier = pltpu.get_barrier_semaphore()
    greeted = x_steps + dp_steps + [s for s in y_steps if s["yh"]]
    for steps in greeted:
        signal(barrier, steps)
    pl.semaphore_wait(barrier, len(greeted))

    class Gather:
        def __init__(self, pack, landing, weights):
            self.pack, self.landing, self.w = pack, landing, weights
            self.sib = wire.copy(pack.at[1 - c], landing, c=1)
            own = weights.at[x, z, yl]
            self.low = wire.copy(own, own, yl=1)
            a, b = weights.at[x, z, 0], weights.at[x, z, 1]
            self.one = (
                [wire.copy(a, a, **s) for s in z_steps],
                [wire.copy(b, b, **s) for s in x_steps],
            )
            a, b = weights.at[x, :, 0], weights.at[:, z, 1]
            self.two = (
                [wire.copy(a, a, x=s) for s in (1, 3)],
                [wire.copy(b, b, z=s) for s in (1, 3)],
            )
            left, right = lax.rem(x + 3, 4), lax.rem(x + 1, 4)
            a, b = weights.at[left, 0:2, 0], weights.at[right, 2:4, 0]
            under, over = lax.rem(z + 3, 4), lax.rem(z + 1, 4)
            d, e = weights.at[0:2, under, 1], weights.at[2:4, over, 1]
            self.pass_x = [wire.copy(a, a, x=1), wire.copy(b, b, x=3)]
            self.pass_z = [wire.copy(d, d, z=1), wire.copy(e, e, z=3)]

        def unit(self):
            self.sib.wait_recv()
            mine = self.pack[c].astype(f32)
            other = self.landing[...].astype(f32)
            first = jnp.where(c == 0, mine, other)[:HD]
            second = jnp.where(c == 0, other, mine)[:HD]
            self.w[x, z, yl] = jnp.concatenate([first, second], axis=0).astype(bf)
            self.low.start()

            @pl.when(yl == 0)
            def _():
                start(self.one[0])

            @pl.when(yl == 1)
            def _():
                start(self.one[1])

        def other_unit(self):
            self.low.wait_recv()

            @pl.when(yl == 0)
            def _():
                start(self.one[1])

            @pl.when(yl == 1)
            def _():
                start(self.one[0])

        def spread(self, kind):
            recv(self.one[kind])
            start(self.two[kind])

        def forward(self):
            for k in (0, 1):
                self.two[0][k].wait_recv()
                self.pass_x[k].start()
                self.two[1][k].wait_recv()
                self.pass_z[k].start()

        def end(self):
            recv(self.pass_x + self.pass_z)
            drain([self.sib, self.low, *self.one[0], *self.one[1]])
            drain([*self.two[0], *self.two[1], *self.pass_x, *self.pass_z])

    class Rows:
        def __init__(self, full):
            own, far = full.at[own_rows], full.at[yhp_rows]
            self.yh = wire.copy(own, own, yh=1)
            self.sib = wire.copy(own, own, c=1)
            self.fwd = wire.copy(far, far, c=1)

        def start(self):
            start([self.yh, self.sib])

        def pass_on(self):
            self.yh.wait_recv()
            self.fwd.start()

        def end(self):
            recv([self.sib, self.fwd])
            drain([self.sib, self.fwd, self.yh])

    class Sums:
        def __init__(self, total, cut_s, cut_y, got_s, got_y):
            self.total, self.cut_s, self.cut_y = total, cut_s, cut_y
            self.got_s, self.got_y = got_s, got_y
            self.sib = wire.copy(cut_s, got_s, c=1)
            self.yh = wire.copy(cut_y, got_y, yh=1)

        def pass_on(self):
            self.sib.wait_recv()
            far = self.total[far_half] + self.got_s[far_half].astype(f32)
            self.cut_y[...] = far.astype(bf)
            self.yh.start()

        def end(self):
            self.yh.wait_recv()
            own = self.total[near_half] + self.got_s[near_half].astype(f32)
            drain([self.sib, self.yh])
            return own + self.got_y[...].astype(f32)

    class Scatter:
        def __init__(self, grads, final, x4, z4, z1, x1, low):
            self.g, self.final, self.low_in = grads, final, low
            self.x4, self.z4, self.z1, self.x1 = x4, z4, z1, x1
            self.one, self.pieces = [], []

        def later(self):
            g = self.g
            self.two = (
                [wire.copy(g.at[x, lax.rem(z + s, 4), 0], self.z1(s - 1), z=s) for s in (1, 2, 3)],
                [wire.copy(g.at[lax.rem(x + s, 4), z, 1], self.x1(s - 1), x=s) for s in (1, 2, 3)],
            )
            self.low = wire.copy(g.at[x, z, 1 - yl], self.low_in, yl=1)
            self.sib = wire.copy(self.final.at[c], self.final.at[c], c=1)

        def piece(self, at):
            copies = []
            for s in (1, 2, 3):
                src = self.g.at[lax.rem(x + s, 4), :, 0, :, at]
                copies.append(wire.copy(src, self.x4(s - 1).at[:, :, at], x=s))
                src = self.g.at[:, lax.rem(z + s, 4), 1, :, at]
                copies.append(wire.copy(src, self.z4(s - 1).at[:, :, at], z=s))
            self.one += copies
            return copies

        def second(self):
            recv(self.one)

            def add(k, carry):
                total = self.g[x, k, 0].astype(f32)
                for s in range(3):
                    total = total + self.x4(s)[k].astype(f32)
                self.g[x, k, 0] = total.astype(bf)
                total = self.g[k, z, 1].astype(f32)
                for s in range(3):
                    total = total + self.z4(s)[k].astype(f32)
                self.g[k, z, 1] = total.astype(bf)
                return carry

            lax.fori_loop(0, 4, add, 0)
            start(self.two[0] + self.two[1])

        def third(self):
            recv(self.two[0] + self.two[1])
            for t, got in ((0, self.z1), (1, self.x1)):
                total = self.g[x, z, t].astype(f32)
                for s in range(3):
                    total = total + got(s)[...].astype(f32)
                self.g[x, z, t] = total.astype(bf)
            self.low.start()

        def fourth(self):
            self.low.wait_recv()
            self.final[c] = self.g[x, z, yl].astype(f32) + self.low_in[...].astype(f32)
            self.sib.start()

        def end(self):
            self.sib.wait_recv()
            drain([*self.one, *self.two[0], *self.two[1], self.low, self.sib])

    w_a = Gather(pack_a, in_pack_a, wa)
    w_m = Gather(pack_m, in_pack_m, wm)
    rows_a, rows_c, rows_m, rows_g = Rows(f_a), Rows(f_c), Rows(f_m), Rows(f_g)
    here = 2 * pair + c
    tile_copies = [wire.copy(tiles.at[here], tiles.at[here], **s) for s in dp_steps]
    strip_copies = [wire.copy(strips.at[x], strips.at[x], **s) for s in x_steps]

    def there(steps):
        far_pair = 2 * lax.rem(z + steps["z"], 4) + lax.rem(yl + steps["yl"], 2)
        return far_pair, lax.rem(c + steps["c"], 2)

    tb_copies = [
        wire.copy(tb_out.at[there(s)[0], there(s)[1]], tb_in.at[k], **s)
        for k, s in enumerate(dp_steps)
    ]
    tb_x = [wire.copy(tb.at[x], tb.at[x], **s) for s in x_steps]

    w_a.sib.start()
    cot_copy = pltpu.make_async_copy(cot_ref, gtok_ref, local)
    cot_copy.start()
    shares_sum = sh_ref[0]
    for k in range(1, 16):
        shares_sum = shares_sum + sh_ref[k]
    share = jnp.full((1, 1), (sh_ref[place] * 16).astype(f32))
    share = share / jnp.full((1, 1), shares_sum.astype(f32))
    present = jnp.where(x < gc_ref[0], 1.0, 0.0)
    facts = (gb_ref[0].astype(f32), gh_ref[x].astype(f32), gw_ref[x].astype(f32), present)
    height, width, live = (jnp.full((1, 1), f) for f in facts[1:])
    for k in range(4):
        tiles[here, k : k + 1] = jnp.full((1, 128), facts[k])
    start(tile_copies)
    strips[x] = jnp.zeros((8, STRIP), f32)
    table = jnp.where(c == 0, bt_ref[0:1], bt_ref[1:2])
    for a in range(39):
        strips[x, a % 2 : a % 2 + 1, 40 * (a // 2) : 40 * (a // 2) + 39] = table[:, 39 * a : 39 * a + 39]
    strips[x, 2:3, 0:288] = jnp.where(c == 0, eb_ref[:, 0:288], eb_ref[:, 288:576])
    w_a.unit()
    unit_a, _ = normalised(tok_ref[...])
    f_a[own_rows] = unit_a.astype(bf)
    rows_a.start()
    start(strip_copies)
    w_m.sib.start()

    time_in = pltpu.roll(te_ref[...], lax.rem(D - HD * place, D), axis=1)[:, 0:HD].astype(bf)
    pieces = [tw_ref[i][:, HD * k : HD * k + HD].astype(f32) for k in (0, 1) for i in (0, 1)]
    by_bucket = dot(time_in, jnp.concatenate(pieces, axis=1).astype(bf))
    position = lax.broadcasted_iota(jnp.int32, (OWN, 1), 0).astype(f32)
    position = position + (yh * OWN).astype(f32)
    valid = jnp.where((position < height * width) & (live > 0.5), 1.0, 0.0)
    cot_copy.wait()
    gtok_ref[...] = gtok_ref[...] * share * valid
    f_c[own_rows] = gtok_ref[...].astype(bf)
    w_a.other_unit()

    recv(tile_copies)
    drain(tile_copies)
    bucket = jnp.concatenate([tiles[d, 0:1, 0:32] for d in range(16)], axis=0)
    is_bucket = bucket == lax.broadcasted_iota(jnp.int32, (16, 32), 1).astype(f32)
    is_bucket = jnp.where(is_bucket, 1.0, 0.0).astype(bf)
    t16[...] = dot(is_bucket, time_in).astype(bf)
    high = by_bucket.astype(bf)
    rest = (by_bucket - high.astype(f32)).astype(bf)
    by_group = dot(is_bucket, high) + dot(is_bucket, rest)
    tb_out[...] = jnp.zeros_like(tb_out)
    for p in range(8):
        for k in (0, 1):
            tb_out[p, k, 0:2, 0:UNIT] = by_group[2 * p : 2 * p + 2, UNIT * k : UNIT * k + UNIT]
    start(tb_copies)
    w_a.spread(0)
    w_a.spread(1)
    w_m.unit()
    rows_a.pass_on()
    rows_c.start()
    for g in (0, 1):
        cell_maps(
            *(tiles[2 * pair + g, k : k + 1, 0:1] for k in (1, 2, 3)),
            to_cells.at[g],
            to_rows.at[g],
            masks.at[g],
        )
    recv(strip_copies)
    drain(strip_copies)

    lane = lax.broadcasted_iota(jnp.int32, (1, STRIP), 1)
    even = lane - 40 * ((lane * 1639) >> 16) < SIDE

    def build_bias(hd, carry):
        for j in range(SIDE):
            one = pltpu.roll(strips[hd, 0:1], STRIP - (19 - j), axis=1)
            two = pltpu.roll(strips[hd, 1:2], (STRIP + SIDE - (19 - j)) % STRIP, axis=1)
            strip[j : j + 1] = jnp.where(even, one, two)
        for i in range(SIDE):
            off = SIDE * (SIDE - 1 - i)
            bias[hd, SIDE * i : SIDE * i + SIDE, :] = strip[0:SIDE, off : off + CELLS]
        return carry

    lax.fori_loop(0, 2, build_bias, 0)
    w_m.other_unit()
    recv(tb_copies)
    total = tb_out[pair, c]
    for k in range(15):
        total = total + tb_in[k]
    tb[x] = total
    drain(tb_copies)
    start(tb_x)
    lax.fori_loop(2, 4, build_bias, 0)
    rows_a.end()
    w_a.forward()
    w_m.spread(0)
    w_m.spread(1)
    rows_c.pass_on()
    recv(tb_x)
    drain(tb_x)
    w_a.end()

    row_id = lax.broadcasted_iota(jnp.int32, (16, 128), 0)
    lane_id = lax.broadcasted_iota(jnp.int32, (16, 128), 1)
    pick = jnp.where(lane_id == row_id + (LANE_P - 128), 1.0, 0.0).astype(bf)
    params = dot_nt(pick, wa[0].reshape(D, FIRST)[:, 128:256])
    par = [params[k : k + 1] for k in range(6)]

    def gain_rows(i, carry):
        at = pl.ds(pl.multiple_of(i * 64, 64), 64)
        f_a[at] = (f_a[at].astype(f32) * par[0] + par[1]).astype(bf)
        return carry

    lax.fori_loop(0, ROWS // 64, gain_rows, 0)

    lanes256 = lax.broadcasted_iota(jnp.int32, (1, 256), 1)

    def head_forward(hd, carry):
        qkv = dot(f_a[...], wa[hd].reshape(D, FIRST))
        for g in (0, 1):
            time_g = tb[hd, g : g + 1]
            low = (qkv[PAD * g : PAD * g + PAD] + jnp.where(lanes256 < HD, time_g, 0.0)).astype(bf)
            cell = dot(to_cells[g], low).astype(bf)
            cells[2 * hd + g] = cell
            score = dot_nt(cell[:, 0:HD], cell[:, HD : 2 * HD]) * SCALE + bias[hd] + masks[g]
            score = jnp.exp(score - jnp.max(score, axis=-1, keepdims=True))
            prob = (score * (1.0 / jnp.sum(score, axis=-1, keepdims=True))).astype(bf)
            probs[2 * hd + g] = prob
            o = dot(to_rows[g], dot(prob, cell[:, 2 * HD : 3 * HD]).astype(bf))
            mixed[hd, PAD * g : PAD * g + PAD, :] = (o + time_g[:, HD : 2 * HD]).astype(bf)
        return carry

    lax.fori_loop(0, 3, head_forward, 0)
    rows_c.end()
    w_m.forward()
    lax.fori_loop(3, 4, head_forward, 0)
    w_m.end()
    for hd in range(4):
        at = HD * hd
        wo[:, at : at + 64] = wm[hd].reshape(D, SECOND)[:, LANE_W:SECOND]
        wo[:, at + 64 : at + HD] = wa[hd].reshape(D, FIRST)[:, LANE_O : LANE_O + 8]
        mixed_all[:, at : at + HD] = mixed[hd]

    def out_project(at):
        return dot_nt(mixed_all[at], wo[...])

    attn_sum = Sums(part, cut_sib, cut_yh, got_sib, got_yh)
    cut_sib[...] = out_project(other_group).astype(bf)
    attn_sum.sib.start()
    part[...] = out_project(own_group)
    attn_sum.pass_on()

    for hd in range(4):
        p, at = hd // 2, 288 * (hd % 2)
        both = wm[hd].reshape(D, SECOND)
        we[p, :, :, at : at + 288] = both[:, 0:288].reshape(8, UNIT, 288)
        wr[p, :, at : at + 288] = both[:, LANE_R : LANE_R + 288]
    out_ref[...] = tok_ref[...] + par[2] + attn_sum.end()
    unit_m, _ = normalised(out_ref[...])
    f_m[own_rows] = (unit_m * par[3] + par[4]).astype(bf)
    rows_m.start()
    rows_m.pass_on()
    rows_m.end()

    def mlp(at):
        total = jnp.zeros((PAD, D), f32)
        for p in (0, 1):
            hidden_bias = jnp.concatenate([strips[2 * p + k, 2:3, 0:288] for k in (0, 1)], axis=1)
            w_e = we[p].reshape(D, 576)
            value, slope = gelu_pair(dot(f_m[at], w_e) + hidden_bias)
            act[p, at] = value.astype(bf)
            low = (dot(f_c[at], wr[p]) * slope).astype(bf)
            gh[p, at] = low
            total = total + dot_nt(low, w_e)
        return total

    mlp_grad = Sums(part, cut_sib, cut_yh, got_sib, got_yh)
    cut_sib[...] = mlp(other_group).astype(bf)
    mlp_grad.sib.start()
    part[...] = mlp(own_group)
    mlp_grad.pass_on()

    def mlp_out(at):
        return dot_nt(act[0, at], wr[0]) + dot_nt(act[1, at], wr[1])

    mlp_sum = Sums(part2, cut_sib2, cut_yh2, got_sib2, got_yh2)
    cut_sib2[...] = mlp_out(other_group).astype(bf)
    mlp_sum.sib.start()
    part2[...] = mlp_out(own_group)

    sc_m = Scatter(
        wm,
        fin_m,
        lambda s: got_x4.at[s],
        lambda s: got_z4.at[s],
        lambda s: got_z1.at[s],
        lambda s: got_x1.at[s],
        got_yl,
    )
    early = sc_m.piece(pl.ds(0, EARLY))
    late = sc_m.piece(pl.ds(EARLY, SECOND - EARLY))
    sc_m.later()
    small[...] = jnp.zeros_like(small)
    ones = jnp.ones((16, ROWS), bf)
    for p in (0, 1):
        bias_sum = dot(ones, gh[p])
        grad_e = dot_tn(f_m[...], gh[p]).astype(bf).reshape(4, 2, UNIT, 576)
        for k in (0, 1):
            hd, at = 2 * p + k, 288 * k
            small[hd, 2:3, 0:288] = bias_sum[0:1, at : at + 288]
            wm[hd, :, :, :, 0:288] = grad_e[:, :, :, at : at + 288]
        grad_r = dot_tn(f_c[...], act[p]).astype(bf).reshape(4, 2, UNIT, 576)
        for k in (0, 1):
            hd, at = 2 * p + k, 288 * k
            wm[hd, :, :, :, LANE_R : LANE_R + 288] = grad_r[:, :, :, at : at + 288]
    start(early)

    unit_m, rstd_m = normalised(out_ref[...])
    gy = mlp_grad.end()
    rgrad[...] = jnp.zeros_like(rgrad)
    rgrad[3:4] = jnp.sum(gy * unit_m, axis=0, keepdims=True)
    rgrad[4:5] = jnp.sum(gy, axis=0, keepdims=True)
    rgrad[5:6] = jnp.sum(f_c[own_rows].astype(f32), axis=0, keepdims=True)
    gtok_ref[...] = gtok_ref[...] + norm_back(gy, par[3], unit_m, rstd_m)
    low_mid = gtok_ref[...].astype(bf)
    rgrad[2:3] = jnp.sum(low_mid.astype(f32), axis=0, keepdims=True)
    f_g[own_rows] = low_mid
    rows_g.start()
    mlp_sum.pass_on()
    rows_g.pass_on()
    bias[...] = jnp.zeros_like(bias)
    rows_g.end()

    grad_mixed = dot(f_g[...], wo[...]).astype(bf)
    grad_o = dot_tn(f_g[...], mixed_all[...]).astype(bf).reshape(4, 2, UNIT, 4 * HD)
    for hd in range(4):
        at = HD * hd
        dqkv[hd, :, 0:HD] = grad_mixed[:, at : at + HD]
        wm[hd, :, :, :, LANE_W:SECOND] = grad_o[:, :, :, at : at + 64]
        wa[hd, :, :, :, LANE_O : LANE_O + 8] = grad_o[:, :, :, at + 64 : at + HD]
    start(late)

    def head_backward(hd, carry):
        for g in (0, 1):
            mine = dqkv[hd, PAD * g : PAD * g + PAD, 0:HD]
            dcell = dot(to_cells[g], mine).astype(bf)
            cell = cells[2 * hd + g]
            prob = probs[2 * hd + g]
            wide = prob.astype(f32)
            dprob = dot_nt(dcell, cell[:, 2 * HD : 3 * HD])
            ds = (wide * (dprob - jnp.sum(dprob * wide, axis=-1, keepdims=True))).astype(bf)
            bias[hd] += ds.astype(f32)
            dq = dot(ds, cell[:, HD : 2 * HD]) * SCALE
            dk = dot_tn(ds, cell[:, 0:HD]) * SCALE
            dv = dot_tn(prob, dcell)
            packed = jnp.concatenate([dq, dk, dv, jnp.zeros((CELLS, 40), f32)], axis=1).astype(bf)
            low = dot(to_rows[g], packed).astype(bf)
            dqkv[hd, PAD * g : PAD * g + PAD, :] = low
            tsum[hd, g : g + 1, 0:HD] = jnp.sum(low[:, 0:HD].astype(f32), axis=0, keepdims=True)
            tsum[hd, g : g + 1, HD : 2 * HD] = jnp.sum(mine.astype(f32), axis=0, keepdims=True)
        return carry

    def rows_backward(hd, carry):
        w_head = wa[hd].reshape(D, FIRST)
        for g in (0, 1):
            totals[g] += dot_nt(dqkv[hd, PAD * g : PAD * g + PAD], w_head)
        return carry

    def weights_backward(hd):
        grad_qkv = dot_tn(f_a[...], dqkv[hd]).astype(bf).reshape(4, 2, UNIT, FIRST)
        wa[hd, :, :, :, 0:LANE_P] = grad_qkv[:, :, :, 0:LANE_P]

    tsum[...] = jnp.zeros_like(tsum)
    lax.fori_loop(0, 2, head_backward, 0)
    out_ref[...] = (out_ref[...] + mlp_sum.end() + par[5]) * valid
    totals[...] = jnp.zeros_like(totals)
    sc_m.second()
    lax.fori_loop(2, 4, head_backward, 0)

    ts_x = [wire.copy(tsum.at[lax.rem(x + s, 4)], got_ts.at[s - 1], x=s) for s in (1, 2, 3)]
    start(ts_x)

    def fold(hd, carry):
        strip[...] = jnp.zeros_like(strip)
        for i in range(SIDE):
            off = SIDE * (SIDE - 1 - i)
            strip[0:SIDE, off : off + CELLS] += bias[hd, SIDE * i : SIDE * i + SIDE, :]
        one = jnp.zeros((1, STRIP), f32)
        two = jnp.zeros((1, STRIP), f32)
        for j in range(SIDE):
            row = strip[j : j + 1]
            one = one + pltpu.roll(jnp.where(even, row, 0.0), 19 - j, axis=1) if j < 19 else (
                one + jnp.where(even, row, 0.0)
            )
            shift = (STRIP + 19 - j - SIDE) % STRIP
            two = two + pltpu.roll(jnp.where(even, 0.0, row), shift, axis=1)
        small[hd, 0:1] = one
        small[hd, 1:2] = two
        return carry

    lax.fori_loop(0, 4, rows_backward, 0)
    attn_grad = Sums(totals.at[c], cut_sib, cut_yh, got_sib, got_yh)
    cut_sib[...] = totals[1 - c].astype(bf)
    attn_grad.sib.start()

    def lot(p, at, low):
        return we.at[p, pl.ds(at, 4), :, pl.ds(low, FIRST)]

    x4 = [lot(0, 0, 0), lot(0, 4, 0), lot(0, 0, FIRST)]
    z4 = [lot(0, 4, FIRST), lot(1, 0, 0), lot(1, 4, 0)]
    sc_a = Scatter(
        wa,
        fin_a,
        lambda s: x4[s],
        lambda s: z4[s],
        lambda s: we.at[1, s, :, pl.ds(FIRST, FIRST)],
        lambda s: we.at[1, s + 3, :, pl.ds(FIRST, FIRST)],
        we.at[1, 6, :, pl.ds(FIRST, FIRST)],
    )
    to_x = [wire.copy(wa.at[lax.rem(x + s, 4), :, 0], x4[s - 1], x=s) for s in (1, 2, 3)]
    sc_a.one += to_x
    for hd in range(4):
        weights_backward(hd)
        for s in (1, 2, 3):
            pl.when(lax.rem(x + s, 4) == hd)(to_x[s - 1].start)
        to_z = [
            wire.copy(wa.at[hd, lax.rem(z + s, 4), 1], z4[s - 1].at[hd], z=s) for s in (1, 2, 3)
        ]
        start(to_z)
        sc_a.one += to_z
        if hd == 0:
            sc_m.third()
        if hd == 1:
            attn_grad.pass_on()
    sc_a.later()
    lax.fori_loop(0, 4, fold, 0)
    small_x = [
        wire.copy(small.at[lax.rem(x + s, 4)], got_small.at[s - 1], x=s) for s in (1, 2, 3)
    ]
    start(small_x)
    sc_m.fourth()

    recv(ts_x)
    drain(ts_x)
    tall[here] = tsum[x] + got_ts[0] + got_ts[1] + got_ts[2]
    tall_copies = [wire.copy(tall.at[here], tall.at[here], **s) for s in dp_steps]
    start(tall_copies)
    unit_a, rstd_a = normalised(tok_ref[...])
    gy = attn_grad.end()
    rgrad[0:1] = jnp.sum(gy * unit_a, axis=0, keepdims=True)
    rgrad[1:2] = jnp.sum(gy, axis=0, keepdims=True)
    rg_x = [wire.copy(rgrad, got_rg.at[s - 1], x=s) for s in (1, 2, 3)]
    start(rg_x)
    gtok_ref[...] = gtok_ref[...] + norm_back(gy, par[0], unit_a, rstd_a)

    sc_a.second()
    recv(small_x)
    drain(small_x)
    small[x] = small[x] + got_small[0] + got_small[1] + got_small[2]
    small_z = [wire.copy(small.at[x], got_small.at[s + 2], z=s) for s in (1, 2, 3)]
    start(small_z)
    recv(rg_x)
    drain(rg_x)
    rgrad[...] = rgrad[...] + got_rg[0] + got_rg[1] + got_rg[2]
    rg_z = [wire.copy(rgrad, got_rg.at[s + 2], z=s) for s in (1, 2, 3)]
    start(rg_z)
    sc_m.end()
    kept = pl.ds(pl.multiple_of(HD * c, 8), HD)
    for k in (0, 1):
        mine = fin_m[k, kept]
        g_exp[:, 288 * k : 288 * k + 288] = mine[:, 0:288]
        g_red[:, 288 * k : 288 * k + 288] = mine[:, LANE_R : LANE_R + 288]
        g_out[HD * k : HD * k + 64] = mine[:, EARLY:SECOND].T[LANE_W - EARLY :]
    recv(tall_copies)
    drain(tall_copies)
    for k in (0, 1):
        sums = jnp.concatenate([tall[2 * p + k, 0:2] for p in range(8)], axis=0)
        high = sums.astype(bf)
        rest = (sums - high.astype(f32)).astype(bf)
        grad_t = dot_tn(t16[...], high) + dot_tn(t16[...], rest)
        g_time[0, :, HD * k : HD * k + HD] = grad_t[:, 0:HD]
        g_time[1, :, HD * k : HD * k + HD] = grad_t[:, HD : 2 * HD]
    sc_a.third()
    recv(small_z)
    drain(small_z)
    small[x] = small[x] + got_small[3] + got_small[4] + got_small[5]
    small_y = wire.copy(small.at[x], got_small.at[6], yl=1)
    small_y.start()
    recv(rg_z)
    drain(rg_z)
    rgrad[...] = rgrad[...] + got_rg[3] + got_rg[4] + got_rg[5]
    rg_y = [wire.copy(rgrad, got_rg7.at[k], **s) for k, s in enumerate(y_steps)]
    start(rg_y)
    sc_a.fourth()
    small_y.wait_recv()
    small_y.wait_send()
    fin_small[c] = small[x] + got_small[6]
    small_c = wire.copy(fin_small.at[c], fin_small.at[c], c=1)
    small_c.start()
    recv(rg_y)
    drain(rg_y)
    total = rgrad[...]
    for k in range(7):
        total = total + got_rg7[k]
    g_rows[...] = pltpu.roll(total, lax.rem(D - HD * place, D), axis=1)[0:6, 0:HD]
    small_c.wait_recv()
    drain([small_c])
    for k in (0, 1):
        g_eb[:, 288 * k : 288 * k + 288] = fin_small[k, 2:3, 0:288]
        for a in range(39):
            at = 40 * (a // 2)
            g_tab[k : k + 1, 39 * a : 39 * a + 39] = fin_small[k, a % 2 : a % 2 + 1, at : at + 39]
    sc_a.end()
    for k in (0, 1):
        mine = fin_a[k, kept]
        for i in range(3):
            g_att[i, :, HD * k : HD * k + HD] = mine[:, HD * i : HD * i + HD]
        g_out[HD * k + 64 : HD * k + HD] = mine[:, 128:256].T[LANE_O - 128 : LANE_O - 120]


def body(
    tokens,
    cotangent,
    time_embed,
    attend_weight,
    time_weight,
    out_weight,
    expand_weight,
    reduce_weight,
    row_params,
    expand_bias,
    bias_table,
    grid_height,
    grid_width,
    group_count,
    group_bucket,
    shares,
):
    vmem = pl.BlockSpec(memory_space=pltpu.VMEM)

    def shape(*dims, kind=bf):
        return pltpu.VMEM(dims, kind)

    scratch = [
        shape(2, 80, FIRST),
        shape(2, 80, SECOND),
        shape(2, UNIT, FIRST, kind=f32),
        shape(2, UNIT, SECOND, kind=f32),
        shape(2, 8, STRIP, kind=f32),
        shape(4, 4, 2, UNIT, FIRST),
        shape(4, 4, 2, UNIT, SECOND),
        shape(80, FIRST),
        shape(80, SECOND),
        shape(16, 8, 128, kind=f32),
        shape(16, HD),
        shape(8, 2, 8, 256, kind=f32),
        shape(15, 8, 256, kind=f32),
        shape(4, 8, 256, kind=f32),
        shape(4, 8, STRIP, kind=f32),
        shape(ROWS, D),
        shape(ROWS, D),
        shape(ROWS, D),
        shape(ROWS, D),
        shape(2, CELLS, PAD),
        shape(2, PAD, CELLS),
        shape(2, 1, CELLS, kind=f32),
        shape(8, CELLS, 256),
        shape(8, CELLS, CELLS),
        shape(24, STRIP, kind=f32),
        shape(4, CELLS, CELLS, kind=f32),
        shape(4, ROWS, HD),
        shape(ROWS, 4 * HD),
        shape(D, 4 * HD),
        shape(4, ROWS, 256),
        shape(2, 8, UNIT, 576),
        shape(2, D, 576),
        shape(2, ROWS, 576),
        shape(2, ROWS, 576),
        shape(2, PAD, D, kind=f32),
        shape(PAD, D),
        shape(OWN, D),
        shape(PAD, D),
        shape(OWN, D),
        shape(PAD, D),
        shape(OWN, D),
        shape(PAD, D),
        shape(OWN, D),
        shape(3, 4, UNIT, SECOND),
        shape(3, 4, UNIT, SECOND),
        shape(3, UNIT, SECOND),
        shape(3, UNIT, SECOND),
        shape(UNIT, SECOND),
        shape(4, 8, STRIP, kind=f32),
        shape(7, 8, STRIP, kind=f32),
        shape(8, D, kind=f32),
        shape(6, 8, D, kind=f32),
        shape(7, 8, D, kind=f32),
        shape(4, 8, 256, kind=f32),
        shape(3, 8, 256, kind=f32),
        shape(16, 8, 256, kind=f32),
        pltpu.SemaphoreType.DMA((N_SEMS,)),
        pltpu.SemaphoreType.DMA((N_SEMS,)),
        pltpu.SemaphoreType.DMA,
    ]
    smem = pl.BlockSpec(memory_space=pltpu.SMEM)
    dims = [
        (OWN, D),
        (OWN, D),
        (3, HD, 2 * HD),
        (2, HD, 2 * HD),
        (2 * HD, HD),
        (HD, 576),
        (HD, 576),
        (6, HD),
        (1, 576),
        (2, 1521),
    ]
    out, gtok, *grads = pl.pallas_call(
        layer_kernel,
        out_shape=[jax.ShapeDtypeStruct(d, f32) for d in dims],
        in_specs=[smem] * 5 + [vmem, pl.BlockSpec(memory_space=pl.ANY)] + [vmem] * 9,
        out_specs=[vmem] * 10,
        scratch_shapes=scratch,
        compiler_params=pltpu.CompilerParams(
            collective_id=0, has_side_effects=True, vmem_limit_bytes=63 * 2**20
        ),
    )(
        grid_height,
        grid_width,
        group_count,
        group_bucket,
        shares,
        tokens,
        cotangent,
        time_embed,
        attend_weight[0],
        time_weight[0],
        out_weight[0],
        expand_weight[0].T,
        reduce_weight[0].T,
        row_params[0],
        expand_bias,
        bias_table[0],
    )
    att, time, outs, expand, reduce, rows, bias, table = grads
    return (
        out,
        gtok,
        att[None],
        time[None],
        outs[None],
        expand.T[None],
        reduce.T[None],
        rows[None],
        bias,
        table[None],
    )


def solution(mesh):
    torus = Mesh(mesh.devices.reshape(tuple(SIZES[a] for a in AXES)), AXES)
    rows = P(DP + MP, None)
    in_specs = (
        rows,
        rows,
        P(),
        P(None, None, DP, MP),
        P(None, None, DP, MP),
        P(None, MP, DP),
        P(None, MP, DP),
        P(None, MP, DP),
        P(None, None, DP),
        P(None, MP),
        P(None, MP, None),
        P(DP),
        P(DP),
        P(DP),
        P(DP),
        P(),
    )
    out_specs = (
        rows,
        rows,
        P(None, None, DP, MP),
        P(None, None, DP, MP),
        P(None, MP, DP),
        P(None, MP, DP),
        P(None, MP, DP),
        P(None, None, DP),
        P(None, MP),
        P(None, MP, None),
    )
    return jax.shard_map(body, mesh=torus, in_specs=in_specs, out_specs=out_specs, check_vma=False)
```
